32 devices in a mesh: grp: 4 (over x, core), mem: 8 (over z, y).
Axes of the slice: x: 2, y: 2, z: 4, core: 2. Of those that a mesh axis runs over, the one named last changes fastest.
Arguments:
- frames: bfloat16 [512, 256, 1024], P('grp', 'mem'), may hold values from -6 to 6
- probe_wave: float32 [2, 128, 128], P(None, 'mem'), may hold values from -6 to 6
Outputs:
- deconv_real: float32 [512, 256, 1024], P('mem', 'grp')
- deconv_imag: float32 [512, 256, 1024], P('mem', 'grp')
The draws below stay inside these ranges and needn't reach their ends.
All inputs are finite; a program needn't handle non-finite values.
Results may differ from the reference program's by a relative error of at most 0.0087.
Values may be sent and summed in bfloat16 or wider, within the bound.
No kernel may reach another device: no remote copies, remote signals or barrier semaphores. Data moves between devices by JAX's collectives and lax.ppermute only.
A program may use at most 256 MiB of HBM per device.

```python
import math
import jax
import jax.numpy as jnp
from jax import lax

WIN = 32
SCAN_Y = 512
SCAN_X = 256
PIX = 1024
PROBE_N = 128
STRIDE_Y = 4
STRIDE_X = 2


def block_scale(key, shape, split, smallest, largest):
    factor_of = 1.0
    for dim, blocks in split:
        steps = jax.random.uniform(jax.random.fold_in(jax.random.fold_in(key, 6), dim), (blocks,), jnp.float32, smallest / len(split), largest / len(split))
        factor_of = factor_of * jnp.repeat(jnp.exp(steps), shape[dim] // blocks).reshape((-1,) + (1,) * (len(shape) - 1 - dim))
    return factor_of


def normal_values(own_key, extent, width, reach, split=(), kind=jnp.bfloat16):
    entries = width * jax.random.normal(own_key, extent, jnp.float32)
    if split:
        entries = entries * block_scale(own_key, extent, split, -0.22, 0.18)
    return jnp.clip(entries, -reach, reach).astype(kind)


def setup_inputs(seed: int = 0) -> dict:
    key_list = jax.random.split(jax.random.key(seed), 3)
    return {
        "frames": normal_values(key_list[0], (SCAN_Y, SCAN_X, PIX), 1.0, 6.0, ((0, 4), (1, 8))),
        "probe_wave": normal_values(key_list[1], (2, PROBE_N, PROBE_N), 1.0, 6.0, ((1, 8),), jnp.float32),
    }


wiener_floor = 0.5

def scan_table(length):
    positions = jnp.arange(length, dtype=jnp.int32)
    phases = positions[:, None] * positions[None, :] % length
    angles = -2.0 * math.pi / length * phases.astype(jnp.float32)
    factor = 1.0 / math.sqrt(length)
    return ((jnp.cos(angles) * factor).astype(jnp.bfloat16), (jnp.sin(angles) * factor).astype(jnp.bfloat16))

def detector_parts(window):
    offsets = jnp.arange(window, dtype=jnp.int32)
    phases = (offsets[:, None, None, None] * offsets[None, None, :, None] + offsets[None, :, None, None] * offsets[None, None, None, :]) % window
    phases = phases.reshape(window * window, window * window)
    angles = -2.0 * math.pi / window * phases.astype(jnp.float32)
    factor = 1.0 / window
    return ((jnp.cos(angles) * factor).astype(jnp.bfloat16), (jnp.sin(angles) * factor).astype(jnp.bfloat16))

def slab_table_of(part_re, part_im):
    upper = jnp.concatenate([part_re, part_im], axis=1)
    lower = jnp.concatenate([-part_im, part_re], axis=1)
    return jnp.concatenate([upper, lower], axis=0)

def signed_shift(freqs, length, step_size):
    centred = jnp.where(freqs >= length // 2, freqs - length, freqs)
    return jnp.floor_divide(centred, step_size).astype(jnp.int32)

def wigner_slab(probe_real, probe_imag, shift_y, shift_x, slab_table):
    grid_size = probe_real.shape[0]
    offsets = jnp.arange(WIN, dtype=jnp.int32)
    row_index = (offsets[None, :] + shift_y[:, None]) % grid_size
    col_index = (offsets[None, :] + shift_x[:, None]) % grid_size
    count_y = shift_y.shape[0]
    count_x = shift_x.shape[0]

    def shifted(plane):
        picked = jnp.take(plane, row_index, axis=0)
        picked = jnp.take(picked, col_index, axis=2)
        return picked.transpose(0, 2, 1, 3).reshape(count_y * count_x, WIN * WIN)
    moved_re = shifted(probe_real)
    moved_im = shifted(probe_imag)
    base_re = probe_real[:WIN, :WIN].reshape(1, WIN * WIN)
    base_im = probe_imag[:WIN, :WIN].reshape(1, WIN * WIN)
    prod_re = (base_re * moved_re + base_im * moved_im).astype(jnp.bfloat16)
    prod_im = (base_im * moved_re - base_re * moved_im).astype(jnp.bfloat16)
    stacked = jnp.concatenate([prod_re, prod_im], axis=1)
    slabs = jnp.dot(stacked, slab_table, preferred_element_type=jnp.float32)
    pixels = WIN * WIN
    slab_shape = (count_y, count_x, pixels)
    return (slabs[:, :pixels].reshape(slab_shape), slabs[:, pixels:].reshape(slab_shape))

def deconvolve(spec_re, spec_im, chi_re, chi_im):
    real_part = spec_re.astype(jnp.float32)
    imag_part = spec_im.astype(jnp.float32)
    denominator = chi_re * chi_re + chi_im * chi_im + wiener_floor
    out_re = (real_part * chi_re + imag_part * chi_im) / denominator
    out_im = (imag_part * chi_re - real_part * chi_im) / denominator
    return (out_re, out_im)

def swap_halves(values):
    half_width = values.shape[-1] // 2
    return jnp.concatenate([-values[..., half_width:], values[..., :half_width]], axis=-1)

def reference(frames, probe_wave):
    highest = lax.Precision.HIGHEST
    det_re, det_im = detector_parts(WIN)
    cy_re, cy_im = scan_table(SCAN_Y)
    cx_re, cx_im = scan_table(SCAN_X)
    cy_re32 = cy_re.astype(jnp.float32)
    cy_im32 = cy_im.astype(jnp.float32)
    cx_re32 = cx_re.astype(jnp.float32)
    cx_im32 = cx_im.astype(jnp.float32)
    flat_rows = frames.reshape(SCAN_Y * SCAN_X, PIX)
    column_groups = 8
    group_width = PIX // column_groups
    re_cols = det_re.reshape(PIX, column_groups, group_width).transpose(1, 0, 2)
    im_cols = det_im.reshape(PIX, column_groups, group_width).transpose(1, 0, 2)

    def one_block(columns):
        cols_re, cols_im = columns
        merged = jnp.concatenate([cols_re, cols_im], axis=1)
        spatial = jnp.dot(flat_rows, merged, preferred_element_type=jnp.float32).astype(jnp.bfloat16)
        spatial = lax.optimization_barrier(spatial)
        spatial = spatial.reshape(SCAN_Y, SCAN_X, 2 * group_width).astype(jnp.float32)
        along_x = jnp.einsum('yrc,rq->yqc', spatial, cx_re32, precision=highest)
        along_x = along_x + jnp.einsum('yrc,rq->yqc', swap_halves(spatial), cx_im32, precision=highest)
        both = jnp.einsum('rxc,rq->qxc', along_x, cy_re32, precision=highest)
        both = both + jnp.einsum('rxc,rq->qxc', swap_halves(along_x), cy_im32, precision=highest)
        return both.astype(jnp.bfloat16)
    spectra = lax.map(one_block, (re_cols, im_cols))
    spectra = spectra.reshape(column_groups, SCAN_Y, SCAN_X, 2, group_width)
    spec_re = spectra[:, :, :, 0, :].transpose(1, 2, 0, 3).reshape(SCAN_Y, SCAN_X, PIX)
    spec_im = spectra[:, :, :, 1, :].transpose(1, 2, 0, 3).reshape(SCAN_Y, SCAN_X, PIX)
    spec_re = lax.optimization_barrier(spec_re)
    spec_im = lax.optimization_barrier(spec_im)
    spec_re = spec_re.reshape(PROBE_N, STRIDE_Y, SCAN_X, PIX)
    spec_im = spec_im.reshape(PROBE_N, STRIDE_Y, SCAN_X, PIX)
    slab_table = slab_table_of(det_re, det_im)
    shift_x = signed_shift(jnp.arange(PROBE_N, dtype=jnp.int32) * STRIDE_X, SCAN_X, STRIDE_X)
    group_ids = jnp.arange(PROBE_N, dtype=jnp.int32)

    def one_group(inputs):
        group_index, rows_re, rows_im = inputs
        shift_y = signed_shift(group_index[None] * STRIDE_Y, SCAN_Y, STRIDE_Y)
        chi_re, chi_im = wigner_slab(probe_wave[0], probe_wave[1], shift_y, shift_x, slab_table)
        chi_re = jnp.repeat(chi_re, STRIDE_X, axis=1)
        chi_im = jnp.repeat(chi_im, STRIDE_X, axis=1)
        return deconvolve(rows_re, rows_im, chi_re, chi_im)
    out_re, out_im = lax.map(one_group, (group_ids, spec_re, spec_im))
    return (out_re.reshape(SCAN_Y, SCAN_X, PIX), out_im.reshape(SCAN_Y, SCAN_X, PIX))
```

```python
import math

import jax
import jax.numpy as jnp
import numpy as np
from jax import lax
from jax.experimental import pallas as pl
from jax.experimental.pallas import tpu as pltpu
from jax.sharding import PartitionSpec as P
import ml_dtypes

WIN = 32
STRIDE_Y = 4
STRIDE_X = 2
LANES = 128
U_TILE = 16
VMEM_BYTES = 56 * 1024 * 1024

wiener_floor = 0.5


def rounded(values):
    return values.astype(np.float32).astype(ml_dtypes.bfloat16)


def scan_table(length):
    positions = np.arange(length)
    angles = -2.0 * math.pi / length * (positions[:, None] * positions[None, :] % length)
    factor = 1.0 / math.sqrt(length)
    return rounded(np.cos(angles) * factor), rounded(np.sin(angles) * factor)


def detector_parts(window):
    offsets = np.arange(window)
    phases = (
        offsets[:, None, None, None] * offsets[None, None, :, None]
        + offsets[None, :, None, None] * offsets[None, None, None, :]
    ) % window
    angles = -2.0 * math.pi / window * phases.reshape(window * window, window * window)
    factor = 1.0 / window
    return rounded(np.cos(angles) * factor), rounded(np.sin(angles) * factor)


def y_table(length, owners):
    t_re, t_im = scan_table(length)
    both = np.stack([t_re.T, t_im.T], axis=0).reshape(2, owners, length // owners, length)
    return both.transpose(1, 0, 2, 3).reshape(2 * length, length)


def x_table(length, owners, senders, x_parts):
    t_re, t_im = scan_table(length)
    upper = np.stack([t_re.T, -t_im.T], axis=1)
    lower = np.stack([t_im.T, t_re.T], axis=1)
    both = np.stack([upper, lower], axis=0)
    width = length // owners
    both = both.reshape(2, owners, width, 2, senders, x_parts, length // senders // x_parts)
    both = both.transpose(1, 0, 2, 3, 5, 4, 6)
    return both.reshape(owners, 2 * width, 2 * length)


def pixel_table(window, depth):
    d_re, d_im = detector_parts(window)
    pixels = window * window
    upper = np.concatenate([d_re, d_im], axis=1).reshape(pixels // depth, depth, 2 * pixels)
    lower = np.concatenate([-d_im, d_re], axis=1).reshape(pixels // depth, depth, 2 * pixels)
    return np.stack([upper, lower], axis=1).reshape(pixels // depth, 2 * depth, 2 * pixels)


def params():
    return pltpu.CompilerParams(vmem_limit_bytes=VMEM_BYTES)


def y_transform(table, pieces, owners, u_chunks):
    n_x, n_y, depth = pieces[0].shape
    per_owner = table.shape[0] // owners
    u_own = per_owner // 2
    step = 2

    def body(t_ref, *refs):
        ins, outs = refs[: len(pieces)], refs[len(pieces) :]
        cols = []
        for i in range(step):
            cols.append(jnp.concatenate([p[i] for p in ins], axis=0))
        if depth == LANES:
            rhs = jnp.concatenate(cols, axis=1)
            res = jnp.dot(t_ref[...], rhs, preferred_element_type=jnp.float32)
            parts = [res[:, i * depth : (i + 1) * depth] for i in range(step)]
        else:
            parts = [jnp.dot(t_ref[...], c, preferred_element_type=jnp.float32) for c in cols]
        for i in range(step):
            res = parts[i].astype(jnp.bfloat16)
            for o_ref, (first, count) in zip(outs, u_chunks):
                for d in range(owners):
                    for r in range(2):
                        row = d * per_owner + r * u_own + first
                        o_ref[d, i, r * count : (r + 1) * count, :] = res[row : row + count]

    out_shape = [
        jax.ShapeDtypeStruct((owners, n_x, 2 * count, depth), jnp.bfloat16) for _, count in u_chunks
    ]
    flops = 2 * table.shape[0] * table.shape[1] * n_x * depth
    moved = 2 * n_x * depth * (table.shape[0] + table.shape[1]) + 2 * table.size
    return pl.pallas_call(
        body,
        grid=(n_x // step,),
        in_specs=[pl.BlockSpec(table.shape, lambda s: (0, 0))]
        + [pl.BlockSpec((step, n_y, depth), lambda s: (s, 0, 0)) for _ in pieces],
        out_specs=[
            pl.BlockSpec((owners, step, 2 * count, depth), lambda s: (0, s, 0, 0))
            for _, count in u_chunks
        ],
        out_shape=out_shape,
        compiler_params=params(),
        cost_estimate=pl.CostEstimate(flops=flops, bytes_accessed=moved, transcendentals=0),
        name="y_transform",
    )(table, *pieces)


def x_transform(table, parts, owners):
    senders, width, rows, depth = parts[0].shape
    n_u = rows // 2
    v_own = table.shape[0] // owners // 2
    views = [p.reshape(senders * width, 2, n_u, depth) for p in parts]
    pair = 2

    def body(t_ref, *refs):
        ins, outs = refs[: len(views)], refs[len(views) :]
        turned = [[jnp.swapaxes(p[:, r], 0, 1) for p in ins] for r in range(2)]
        for u in range(0, U_TILE, pair):
            cols = [
                jnp.concatenate([turned[r][h][u + i] for r in range(2) for h in range(len(ins))], axis=0)
                for i in range(pair)
            ]
            if depth == LANES:
                rhs = jnp.concatenate(cols, axis=1)
                res = jnp.dot(t_ref[...], rhs, preferred_element_type=jnp.float32)
                made = [res[:, i * depth : (i + 1) * depth] for i in range(pair)]
            else:
                made = [jnp.dot(t_ref[...], c, preferred_element_type=jnp.float32) for c in cols]
            for i in range(pair):
                res = made[i].astype(jnp.bfloat16)
                for d in range(owners):
                    for r in range(2):
                        row = (2 * d + r) * v_own
                        outs[d][u + i, r] = res[row : row + v_own]

    flops = 2 * table.size * n_u * depth
    moved = 4 * sum(p.size for p in parts) + 2 * table.size
    return pl.pallas_call(
        body,
        grid=(n_u // U_TILE,),
        in_specs=[pl.BlockSpec(table.shape, lambda s: (0, 0))]
        + [pl.BlockSpec((senders * width, 2, U_TILE, depth), lambda s: (0, 0, s, 0)) for _ in views],
        out_specs=[
            pl.BlockSpec((U_TILE, 2, v_own, depth), lambda s: (s, 0, 0, 0)) for _ in range(owners)
        ],
        out_shape=[
            jax.ShapeDtypeStruct((n_u, 2, v_own, depth), jnp.bfloat16) for _ in range(owners)
        ],
        compiler_params=params(),
        cost_estimate=pl.CostEstimate(flops=flops, bytes_accessed=moved, transcendentals=0),
        name="x_transform",
    )(table, *views)


def chi_factors(product, table, count_y, v_own):
    rows, inner = product.shape
    pixels = table.shape[1] // 2
    lanes = 256

    def body(p_ref, t_ref, re_ref, im_ref):
        for n in range(pixels // lanes):
            at = slice(n * lanes, (n + 1) * lanes)
            to = slice(pixels + n * lanes, pixels + (n + 1) * lanes)
            c_re = jnp.dot(p_ref[...], t_ref[:, at], preferred_element_type=jnp.float32)
            c_im = jnp.dot(p_ref[...], t_ref[:, to], preferred_element_type=jnp.float32)
            scale = 1.0 / (c_re * c_re + c_im * c_im + wiener_floor)
            re_ref[0, :, at] = c_re * scale
            im_ref[0, :, at] = c_im * scale

    return pl.pallas_call(
        body,
        grid=(count_y,),
        in_specs=[
            pl.BlockSpec((v_own, inner), lambda s: (s, 0)),
            pl.BlockSpec(table.shape, lambda s: (0, 0)),
        ],
        out_specs=[pl.BlockSpec((1, v_own, pixels), lambda s: (s, 0, 0))] * 2,
        out_shape=[jax.ShapeDtypeStruct((count_y, v_own, pixels), jnp.float32)] * 2,
        compiler_params=params(),
        cost_estimate=pl.CostEstimate(
            flops=2 * rows * table.size, bytes_accessed=2 * table.size + 8 * rows * pixels, transcendentals=0
        ),
        name="chi_factors",
    )(product, table)


def pixel_transform(table, early, late, factor_re, factor_im, first, count, total_u, previous):
    inner = table.shape[0]
    pixels = table.shape[1] // 2
    v_own, depth = late[0].shape[2:]
    step = STRIDE_Y
    rows = step * v_own
    lanes = 256
    base = first // step
    n_early, n_late = len(early), len(late)

    def body(t_ref, cr_ref, ci_ref, *refs):
        ins = refs[: n_early + n_late]
        re_ref, im_ref = refs[-2:]
        cuts = [p[:, r].reshape(rows, depth) for p in ins for r in range(2)]
        if depth == LANES:
            cuts = [jnp.concatenate(cuts, axis=1)]
        size = inner // len(cuts)

        def total(at):
            made = None
            for i, cut in enumerate(cuts):
                term = jnp.dot(cut, t_ref[i * size : (i + 1) * size, at], preferred_element_type=jnp.float32)
                made = term if made is None else made + term
            return made.reshape(step, v_own, lanes)

        for n in range(pixels // lanes):
            at = slice(n * lanes, (n + 1) * lanes)
            s_re = total(at)
            s_im = total(slice(pixels + n * lanes, pixels + (n + 1) * lanes))
            c_re = cr_ref[:, :, at]
            c_im = ci_ref[:, :, at]
            re_ref[:, :, at] = s_re * c_re + s_im * c_im
            im_ref[:, :, at] = s_im * c_re - s_re * c_im

    factor_spec = pl.BlockSpec((1, v_own, pixels), lambda s: (base + s, 0, 0))
    out_spec = pl.BlockSpec((step, v_own, pixels), lambda s: (base + s, 0, 0))
    shape = jax.ShapeDtypeStruct((total_u, v_own, pixels), jnp.float32)
    operands = [table, factor_re, factor_im, *early, *late]
    aliases = {}
    for i, array in enumerate(previous):
        aliases[len(operands)] = i
        operands.append(array)
    return pl.pallas_call(
        body,
        grid=(count // step,),
        in_specs=[pl.BlockSpec(table.shape, lambda s: (0, 0)), factor_spec, factor_spec]
        + [pl.BlockSpec((step, 2, v_own, depth), lambda s: (base + s, 0, 0, 0)) for _ in early]
        + [pl.BlockSpec((step, 2, v_own, depth), lambda s: (s, 0, 0, 0)) for _ in late]
        + [pl.BlockSpec(memory_space=pl.ANY) for _ in previous],
        out_specs=[out_spec] * 2,
        out_shape=[shape] * 2,
        input_output_aliases=aliases,
        compiler_params=params(),
        cost_estimate=pl.CostEstimate(
            flops=2 * count * v_own * table.size,
            bytes_accessed=2 * table.size + 12 * count * v_own * pixels,
            transcendentals=0,
        ),
        name="pixel_transform",
    )(*operands)


def signed_shift(freqs, length, step_size):
    centred = jnp.where(freqs >= length // 2, freqs - length, freqs)
    return jnp.floor_divide(centred, step_size)


def probe_product(probe, shift_y, shift_x, repeat, depth):
    grid_size = probe.shape[-1]
    offsets = jnp.arange(WIN, dtype=jnp.int32)
    row_index = (offsets[None, :] + shift_y[:, None]) % grid_size
    col_index = (offsets[None, :] + shift_x[:, None]) % grid_size
    count_y = shift_y.shape[0]
    count_x = shift_x.shape[0]
    pixels = WIN * WIN

    def shifted(plane):
        picked = jnp.take(plane, row_index, axis=0)
        picked = jnp.take(picked, col_index, axis=2)
        return picked.transpose(0, 2, 1, 3).reshape(count_y, count_x, pixels)

    moved_re = shifted(probe[0])
    moved_im = shifted(probe[1])
    base_re = probe[0, :WIN, :WIN].reshape(1, 1, pixels)
    base_im = probe[1, :WIN, :WIN].reshape(1, 1, pixels)
    prod_re = (base_re * moved_re + base_im * moved_im).astype(jnp.bfloat16)
    prod_im = (base_im * moved_re - base_re * moved_im).astype(jnp.bfloat16)
    blocks = []
    for b in range(pixels // depth):
        blocks.append(prod_re[..., b * depth : (b + 1) * depth])
        blocks.append(prod_im[..., b * depth : (b + 1) * depth])
    stacked = jnp.concatenate(blocks, axis=-1)
    stacked = jnp.repeat(stacked, repeat, axis=1)
    return stacked.reshape(count_y * count_x * repeat, 2 * pixels)


def swap(array, partner, size):
    return lax.ppermute(array, "grp", [(i, i ^ partner) for i in range(size)])


def shards(frames, probe_wave):
    n_grp, n_mem = lax.axis_size("grp"), lax.axis_size("mem")
    grp, mem = lax.axis_index("grp"), lax.axis_index("mem")
    n_y, n_x, pixels = frames.shape
    scan_y, scan_x = n_y * n_grp, n_x * n_mem
    u_own, v_own = scan_y // n_mem, scan_x // n_grp
    depth = min(LANES, pixels // n_grp)
    n_q = pixels // (n_grp * depth)
    partners = grp ^ jnp.arange(n_grp, dtype=jnp.int32)
    x_parts = 2 if n_x >= 32 else 1
    width = n_x // x_parts

    if u_own >= 4 * U_TILE:
        sizes = [u_own // 2, u_own // 4, u_own // 4]
    else:
        sizes = [U_TILE] * (u_own // U_TILE)
    late_chunks = []
    for size in sizes:
        late_chunks.append((sum(c for _, c in late_chunks), size))

    whole_probe = lax.all_gather(probe_wave, "mem", axis=1, tiled=True)

    def cut(q, first, count):
        made = []
        for j in range(n_grp):
            at = (q * n_grp + (grp ^ j)) * depth
            piece = lax.dynamic_slice(frames, (0, first, at), (n_y, count, depth))
            made.append(piece.transpose(1, 0, 2))
        return made

    def exchange(pieces):
        return [pieces[0]] + [swap(pieces[j], j, n_grp) for j in range(1, n_grp)]

    def to_owners(array):
        return lax.all_to_all(array, "mem", split_axis=0, concat_axis=0, tiled=True)

    ty = jnp.asarray(y_table(scan_y, n_mem)).reshape(2 * scan_y, n_grp, n_y)
    ty = jnp.take(ty, partners, axis=1).reshape(2 * scan_y, scan_y)
    tx, tx_late = (
        jnp.take(jnp.asarray(x_table(scan_x, n_grp, n_mem, parts)), partners, axis=0).reshape(
            2 * scan_x, 2 * scan_x
        )
        for parts in (x_parts, 1)
    )
    tk_all = jnp.asarray(pixel_table(WIN, depth))
    blocks = (jnp.arange(n_q, dtype=jnp.int32)[:, None] * n_grp + partners[None, :]).reshape(-1)
    tk = jnp.take(tk_all, blocks, axis=0).reshape(2 * pixels, 2 * pixels)
    tk_all = tk_all.reshape(2 * pixels, 2 * pixels)

    fronts = [(q, h * width, width) for q in range(n_q - 1) for h in range(x_parts)]
    fronts.append((n_q - 1, 0, n_x))
    pieces = exchange(cut(*fronts[0]))
    early_sent = []
    ready = None
    for i in range(len(fronts) - 1):
        (ready,) = y_transform(ty, pieces, n_mem, [(0, u_own)])
        following = cut(*fronts[i + 1])
        ready, following = lax.optimization_barrier((ready, following))
        early_sent.append(to_owners(ready))
        pieces = exchange(following)
    late_ready = y_transform(ty, pieces, n_mem, late_chunks)

    shift_y = signed_shift(
        mem * u_own + STRIDE_Y * jnp.arange(u_own // STRIDE_Y, dtype=jnp.int32), scan_y, STRIDE_Y
    )
    shift_x = signed_shift(
        grp * v_own + STRIDE_X * jnp.arange(v_own // STRIDE_X, dtype=jnp.int32), scan_x, STRIDE_X
    )
    product = probe_product(whole_probe, shift_y, shift_x, STRIDE_X, depth)
    factor_re, factor_im = chi_factors(product, tk_all, u_own // STRIDE_Y, v_own)

    early = []
    waiting = [early_sent[q * x_parts : (q + 1) * x_parts] for q in range(n_q - 1)]
    late = []
    for c in range(len(late_chunks)):
        sending = late_ready[c]
        if c == 0:
            sending, waiting = lax.optimization_barrier((sending, waiting))
            arrived = to_owners(sending)
            for parts in waiting:
                early += exchange(x_transform(tx, parts, n_grp))
        else:
            sending, previous = lax.optimization_barrier((sending, arrived))
            arrived = to_owners(sending)
            late.append(exchange(x_transform(tx_late, [previous], n_grp)))
    late.append(exchange(x_transform(tx_late, [arrived], n_grp)))

    outs = []
    for (first, count), pieces in zip(late_chunks, late):
        outs = pixel_transform(tk, early, pieces, factor_re, factor_im, first, count, u_own, outs)
    return tuple(outs)


def solution(mesh):
    return jax.shard_map(
        shards,
        mesh=mesh,
        in_specs=(P("grp", "mem", None), P(None, "mem", None)),
        out_specs=(P("mem", "grp", None), P("mem", "grp", None)),
        check_vma=False,
    )
```

```python
import math

import jax
import jax.numpy as jnp
import numpy as np
from jax import lax
from jax.experimental import pallas as pl
from jax.experimental.pallas import tpu as pltpu
from jax.sharding import PartitionSpec as P
import ml_dtypes

WIN = 32
STRIDE_Y = 4
STRIDE_X = 2
LANES = 128
U_TILE = 16
VMEM_BYTES = 56 * 1024 * 1024

wiener_floor = 0.5


def rounded(values):
    return values.astype(np.float32).astype(ml_dtypes.bfloat16)


def scan_table(length):
    positions = np.arange(length)
    angles = -2.0 * math.pi / length * (positions[:, None] * positions[None, :] % length)
    factor = 1.0 / math.sqrt(length)
    return rounded(np.cos(angles) * factor), rounded(np.sin(angles) * factor)


def detector_parts(window):
    offsets = np.arange(window)
    phases = (
        offsets[:, None, None, None] * offsets[None, None, :, None]
        + offsets[None, :, None, None] * offsets[None, None, None, :]
    ) % window
    angles = -2.0 * math.pi / window * phases.reshape(window * window, window * window)
    factor = 1.0 / window
    return rounded(np.cos(angles) * factor), rounded(np.sin(angles) * factor)


def y_table(length, owners):
    t_re, t_im = scan_table(length)
    both = np.stack([t_re.T, t_im.T], axis=0).reshape(2, owners, length // owners, length)
    return both.transpose(1, 0, 2, 3).reshape(2 * length, length)


def x_table(length, owners, senders, cuts):
    t_re, t_im = scan_table(length)
    upper = np.stack([t_re.T, -t_im.T], axis=1)
    lower = np.stack([t_im.T, t_re.T], axis=1)
    both = np.stack([upper, lower], axis=0)
    width = length // owners
    both = both.reshape(2, owners, width, 2, senders, length // senders).transpose(1, 0, 2, 3, 4, 5)
    parts = [
        both[..., first : first + count].reshape(owners, 2 * width, 2, senders * count)
        for first, count in cuts
    ]
    return np.concatenate(parts, axis=-1).reshape(owners, 2 * width, 2 * length)


def pixel_table(window, depth):
    d_re, d_im = detector_parts(window)
    pixels = window * window
    upper = np.concatenate([d_re, d_im], axis=1).reshape(pixels // depth, depth, 2 * pixels)
    lower = np.concatenate([-d_im, d_re], axis=1).reshape(pixels // depth, depth, 2 * pixels)
    return np.stack([upper, lower], axis=1).reshape(pixels // depth, 2 * depth, 2 * pixels)


def params():
    return pltpu.CompilerParams(vmem_limit_bytes=VMEM_BYTES)


def y_transform(table, pieces, owners, u_chunks):
    n_x, n_y, depth = pieces[0].shape
    per_owner = table.shape[0] // owners
    u_own = per_owner // 2
    step = 2

    def body(t_ref, *refs):
        ins, outs = refs[: len(pieces)], refs[len(pieces) :]
        cols = []
        for i in range(step):
            cols.append(jnp.concatenate([p[i] for p in ins], axis=0))
        if depth == LANES:
            rhs = jnp.concatenate(cols, axis=1)
            res = jnp.dot(t_ref[...], rhs, preferred_element_type=jnp.float32)
            parts = [res[:, i * depth : (i + 1) * depth] for i in range(step)]
        else:
            parts = [jnp.dot(t_ref[...], c, preferred_element_type=jnp.float32) for c in cols]
        for i in range(step):
            res = parts[i].astype(jnp.bfloat16)
            for o_ref, (first, count) in zip(outs, u_chunks):
                for d in range(owners):
                    for r in range(2):
                        row = d * per_owner + r * u_own + first
                        o_ref[d, i, r * count : (r + 1) * count, :] = res[row : row + count]

    out_shape = [
        jax.ShapeDtypeStruct((owners, n_x, 2 * count, depth), jnp.bfloat16) for _, count in u_chunks
    ]
    flops = 2 * table.shape[0] * table.shape[1] * n_x * depth
    moved = 2 * n_x * depth * (table.shape[0] + table.shape[1]) + 2 * table.size
    return pl.pallas_call(
        body,
        grid=(n_x // step,),
        in_specs=[pl.BlockSpec(table.shape, lambda s: (0, 0))]
        + [pl.BlockSpec((step, n_y, depth), lambda s: (s, 0, 0)) for _ in pieces],
        out_specs=[
            pl.BlockSpec((owners, step, 2 * count, depth), lambda s: (0, s, 0, 0))
            for _, count in u_chunks
        ],
        out_shape=out_shape,
        compiler_params=params(),
        cost_estimate=pl.CostEstimate(flops=flops, bytes_accessed=moved, transcendentals=0),
        name="y_transform",
    )(table, *pieces)


def x_transform(table, parts, owners):
    rows, depth = parts[0].shape[2:]
    n_u = rows // 2
    v_own = table.shape[0] // owners // 2
    views = [p.reshape(p.shape[0] * p.shape[1], 2, n_u, depth) for p in parts]
    pair = 2

    def body(t_ref, *refs):
        ins, outs = refs[: len(views)], refs[len(views) :]
        turned = [[jnp.swapaxes(p[:, r], 0, 1) for p in ins] for r in range(2)]
        for u in range(0, U_TILE, pair):
            cols = [
                jnp.concatenate([turned[r][h][u + i] for r in range(2) for h in range(len(ins))], axis=0)
                for i in range(pair)
            ]
            if depth == LANES:
                rhs = jnp.concatenate(cols, axis=1)
                res = jnp.dot(t_ref[...], rhs, preferred_element_type=jnp.float32)
                made = [res[:, i * depth : (i + 1) * depth] for i in range(pair)]
            else:
                made = [jnp.dot(t_ref[...], c, preferred_element_type=jnp.float32) for c in cols]
            for i in range(pair):
                res = made[i].astype(jnp.bfloat16)
                for d in range(owners):
                    for r in range(2):
                        row = (2 * d + r) * v_own
                        outs[d][u + i, r] = res[row : row + v_own]

    flops = 2 * table.size * n_u * depth
    moved = 4 * sum(p.size for p in parts) + 2 * table.size
    return pl.pallas_call(
        body,
        grid=(n_u // U_TILE,),
        in_specs=[pl.BlockSpec(table.shape, lambda s: (0, 0))]
        + [pl.BlockSpec((v.shape[0], 2, U_TILE, depth), lambda s: (0, 0, s, 0)) for v in views],
        out_specs=[
            pl.BlockSpec((U_TILE, 2, v_own, depth), lambda s: (s, 0, 0, 0)) for _ in range(owners)
        ],
        out_shape=[
            jax.ShapeDtypeStruct((n_u, 2, v_own, depth), jnp.bfloat16) for _ in range(owners)
        ],
        compiler_params=params(),
        cost_estimate=pl.CostEstimate(flops=flops, bytes_accessed=moved, transcendentals=0),
        name="x_transform",
    )(table, *views)


def chi_factors(windows, base, table, count_y):
    n_rows, v_own, lanes = windows.shape[1:]
    n_blocks = base.shape[1]
    stride = lanes // WIN
    inner, columns = table.shape
    pixels = columns // 2
    step = min(4, count_y)
    wide = 256

    def body(w_ref, b_ref, t_ref, re_ref, im_ref, left):
        first = pl.program_id(0) * step
        for i in range(step):
            for b in range(n_blocks):
                w_re = w_ref[0, first + i + b * stride]
                w_im = w_ref[1, first + i + b * stride]
                a_re = b_ref[0, b : b + 1]
                a_im = b_ref[1, b : b + 1]
                rows = slice(i * v_own, (i + 1) * v_own)
                at = 2 * b * lanes
                left[rows, at : at + lanes] = (a_re * w_re + a_im * w_im).astype(jnp.bfloat16)
                left[rows, at + lanes : at + 2 * lanes] = (a_im * w_re - a_re * w_im).astype(jnp.bfloat16)
        for n in range(pixels // wide):
            at = slice(n * wide, (n + 1) * wide)
            to = slice(pixels + n * wide, pixels + (n + 1) * wide)
            c_re = jnp.dot(left[...], t_ref[:, at], preferred_element_type=jnp.float32)
            c_im = jnp.dot(left[...], t_ref[:, to], preferred_element_type=jnp.float32)
            scale = 1.0 / (c_re * c_re + c_im * c_im + wiener_floor)
            re_ref[:, :, at] = (c_re * scale).reshape(step, v_own, wide)
            im_ref[:, :, at] = (c_im * scale).reshape(step, v_own, wide)

    rows = count_y * v_own
    return pl.pallas_call(
        body,
        grid=(count_y // step,),
        in_specs=[
            pl.BlockSpec(windows.shape, lambda s: (0, 0, 0, 0)),
            pl.BlockSpec(base.shape, lambda s: (0, 0, 0)),
            pl.BlockSpec(table.shape, lambda s: (0, 0)),
        ],
        out_specs=[pl.BlockSpec((step, v_own, pixels), lambda s: (s, 0, 0))] * 2,
        out_shape=[jax.ShapeDtypeStruct((count_y, v_own, pixels), jnp.float32)] * 2,
        scratch_shapes=[pltpu.VMEM((step * v_own, inner), jnp.bfloat16)],
        compiler_params=params(),
        cost_estimate=pl.CostEstimate(
            flops=2 * rows * table.size, bytes_accessed=2 * table.size + 8 * rows * pixels, transcendentals=0
        ),
        name="chi_factors",
    )(windows, base, table)


def pixel_transform(table, early, late, factor_re, factor_im, first, count, total_u, previous):
    inner = table.shape[0]
    pixels = table.shape[1] // 2
    v_own, depth = late[0].shape[2:]
    step = STRIDE_Y
    rows = step * v_own
    lanes = 256
    base = first // step
    n_early, n_late = len(early), len(late)

    def body(t_ref, cr_ref, ci_ref, *refs):
        ins = refs[: n_early + n_late]
        re_ref, im_ref = refs[-2:]
        cuts = [p[:, r].reshape(rows, depth) for p in ins for r in range(2)]
        if depth == LANES:
            cuts = [jnp.concatenate(cuts, axis=1)]
        size = inner // len(cuts)

        def total(at):
            made = None
            for i, cut in enumerate(cuts):
                term = jnp.dot(cut, t_ref[i * size : (i + 1) * size, at], preferred_element_type=jnp.float32)
                made = term if made is None else made + term
            return made.reshape(step, v_own, lanes)

        for n in range(pixels // lanes):
            at = slice(n * lanes, (n + 1) * lanes)
            s_re = total(at)
            s_im = total(slice(pixels + n * lanes, pixels + (n + 1) * lanes))
            c_re = cr_ref[:, :, at]
            c_im = ci_ref[:, :, at]
            re_ref[:, :, at] = s_re * c_re + s_im * c_im
            im_ref[:, :, at] = s_im * c_re - s_re * c_im

    factor_spec = pl.BlockSpec((1, v_own, pixels), lambda s: (base + s, 0, 0))
    out_spec = pl.BlockSpec((step, v_own, pixels), lambda s: (base + s, 0, 0))
    shape = jax.ShapeDtypeStruct((total_u, v_own, pixels), jnp.float32)
    operands = [table, factor_re, factor_im, *early, *late]
    aliases = {}
    for i, array in enumerate(previous):
        aliases[len(operands)] = i
        operands.append(array)
    return pl.pallas_call(
        body,
        grid=(count // step,),
        in_specs=[pl.BlockSpec(table.shape, lambda s: (0, 0)), factor_spec, factor_spec]
        + [pl.BlockSpec((step, 2, v_own, depth), lambda s: (base + s, 0, 0, 0)) for _ in early]
        + [pl.BlockSpec((step, 2, v_own, depth), lambda s: (s, 0, 0, 0)) for _ in late]
        + [pl.BlockSpec(memory_space=pl.ANY) for _ in previous],
        out_specs=[out_spec] * 2,
        out_shape=[shape] * 2,
        input_output_aliases=aliases,
        compiler_params=params(),
        cost_estimate=pl.CostEstimate(
            flops=2 * count * v_own * table.size,
            bytes_accessed=2 * table.size + 12 * count * v_own * pixels,
            transcendentals=0,
        ),
        name="pixel_transform",
    )(*operands)


def signed_shift(freqs, length, step_size):
    centred = jnp.where(freqs >= length // 2, freqs - length, freqs)
    return jnp.floor_divide(centred, step_size)


def probe_windows(probe, shift_y, shift_x, lanes):
    grid_size = probe.shape[-1]
    stride = lanes // WIN
    count_x = shift_x.shape[0]
    n_rows = shift_y.shape[0] + WIN - stride
    rows = (shift_y[0] + jnp.arange(n_rows + stride - 1, dtype=jnp.int32)) % grid_size
    columns = (shift_x[:, None] + jnp.arange(WIN, dtype=jnp.int32)[None, :]) % grid_size
    picked = jnp.take(probe, rows, axis=1, mode="clip")
    chosen = (jnp.arange(grid_size, dtype=jnp.int32)[:, None] == columns.reshape(1, -1)).astype(jnp.float32)
    moved = jnp.einsum("prc,cm->prm", picked, chosen, precision=lax.Precision.HIGHEST)
    moved = moved.reshape(2, n_rows + stride - 1, count_x, WIN)
    return jnp.concatenate([moved[:, p : p + n_rows] for p in range(stride)], axis=-1)


def swap(array, partner, axis):
    size = lax.axis_size(axis)
    return lax.ppermute(array, axis, [(i, i ^ partner) for i in range(size)])


def gather_rows(block, axis):
    rank = lax.axis_index(axis)
    partner = 1
    while partner < lax.axis_size(axis):
        other = swap(block, partner, axis)
        ahead = (rank & partner) > 0
        block = jnp.concatenate(
            [jnp.where(ahead, other, block), jnp.where(ahead, block, other)], axis=1
        )
        partner *= 2
    return block


def shards(frames, probe_wave):
    n_grp, n_mem = lax.axis_size("grp"), lax.axis_size("mem")
    grp, mem = lax.axis_index("grp"), lax.axis_index("mem")
    n_y, n_x, pixels = frames.shape
    scan_y, scan_x = n_y * n_grp, n_x * n_mem
    u_own, v_own = scan_y // n_mem, scan_x // n_grp
    depth = min(LANES, pixels // n_grp)
    n_q = pixels // (n_grp * depth)
    partners = grp ^ jnp.arange(n_grp, dtype=jnp.int32)
    if n_x >= 32:
        opening = 2 * (n_x * 5 // 32)
        x_cuts = [(0, opening), (opening, n_x - opening)]
    else:
        x_cuts = [(0, n_x)]

    if u_own >= 4 * U_TILE:
        sizes = [u_own // 2, u_own // 4, u_own // 4]
    else:
        sizes = [U_TILE] * (u_own // U_TILE)
    u_chunks = []
    for size in sizes:
        u_chunks.append((sum(c for _, c in u_chunks), size))

    def cut(q, first, count):
        made = []
        for j in range(n_grp):
            at = (q * n_grp + (grp ^ j)) * depth
            piece = lax.dynamic_slice(frames, (0, first, at), (n_y, count, depth))
            made.append(piece.transpose(1, 0, 2))
        return made

    def exchange(pieces):
        return [pieces[0]] + [swap(pieces[j], j, "grp") for j in range(1, n_grp)]

    def to_owners(array):
        return lax.all_to_all(array, "mem", split_axis=0, concat_axis=0, tiled=True)

    def chosen(table, index, axis):
        return jnp.take(jnp.asarray(table), index, axis=axis, mode="clip")

    ty = chosen(y_table(scan_y, n_mem).reshape(2 * scan_y, n_grp, n_y), partners, 1)
    ty = ty.reshape(2 * scan_y, scan_y)

    fronts = [(q, first, count) for q in range(n_q - 1) for first, count in x_cuts]
    fronts.append((n_q - 1, 0, n_x))
    pieces = exchange(cut(*fronts[0]))
    whole_probe = gather_rows(probe_wave, "mem")
    arrived = []
    for i in range(len(fronts) - 1):
        (ready,) = y_transform(ty, pieces, n_mem, [(0, u_own)])
        following = cut(*fronts[i + 1])
        ready, following, whole_probe = lax.optimization_barrier((ready, following, whole_probe))
        arrived.append(to_owners(ready))
        pieces = exchange(following)
    late_ready = y_transform(ty, pieces, n_mem, u_chunks)

    shift_y = signed_shift(
        mem * u_own + STRIDE_Y * jnp.arange(u_own // STRIDE_Y, dtype=jnp.int32), scan_y, STRIDE_Y
    )
    shift_x = signed_shift(grp * v_own + jnp.arange(v_own, dtype=jnp.int32), scan_x, STRIDE_X)
    base = whole_probe[:, :WIN, :WIN].reshape(2, WIN * WIN // LANES, LANES)
    windows = probe_windows(whole_probe, shift_y, shift_x, LANES)
    chi_table = jnp.asarray(pixel_table(WIN, LANES).reshape(2 * pixels, 2 * pixels))
    factors = chi_factors(windows, base, chi_table, u_own // STRIDE_Y)
    tx, tx_late = (
        chosen(x_table(scan_x, n_grp, n_mem, cuts), partners, 0).reshape(2 * scan_x, 2 * scan_x)
        for cuts in (x_cuts, [(0, n_x)])
    )
    blocks = (jnp.arange(n_q, dtype=jnp.int32)[:, None] * n_grp + partners[None, :]).reshape(-1)
    tk = chosen(pixel_table(WIN, depth), blocks, 0).reshape(2 * pixels, 2 * pixels)

    late_ready, arrived, factors, tx, tx_late, tk = lax.optimization_barrier(
        (late_ready, arrived, factors, tx, tx_late, tk)
    )
    last = to_owners(late_ready[0])
    early = []
    for q in range(n_q - 1):
        early += exchange(x_transform(tx, arrived[q * len(x_cuts) : (q + 1) * len(x_cuts)], n_grp))
    late = []
    ahead = early
    outs = []
    for c in range(1, len(u_chunks)):
        sending, last, _ = lax.optimization_barrier((late_ready[c], last, ahead))
        following = to_owners(sending)
        ahead = exchange(x_transform(tx_late, [last], n_grp))
        late.append(ahead)
        last = following
    if len(u_chunks) > 1:
        first, count = u_chunks[0]
        outs = pixel_transform(tk, early, late[0], *factors, first, count, u_own, outs)
        last, _ = lax.optimization_barrier((last, outs[0][0, 0]))
    late.append(exchange(x_transform(tx_late, [last], n_grp)))

    for c in range(min(1, len(u_chunks) - 1), len(u_chunks)):
        first, count = u_chunks[c]
        outs = pixel_transform(tk, early, late[c], *factors, first, count, u_own, outs)
    return tuple(outs)


def solution(mesh):
    return jax.shard_map(
        shards,
        mesh=mesh,
        in_specs=(P("grp", "mem", None), P(None, "mem", None)),
        out_specs=(P("mem", "grp", None), P("mem", "grp", None)),
        check_vma=False,
    )
```

```python
import math

import jax
import jax.numpy as jnp
import numpy as np
from jax import lax
from jax.experimental import pallas as pl
from jax.experimental.pallas import tpu as pltpu
from jax.sharding import PartitionSpec as P
import ml_dtypes

WIN = 32
STRIDE_Y = 4
STRIDE_X = 2
LANES = 128
U_TILE = 8
VMEM_BYTES = 56 * 1024 * 1024

wiener_floor = 0.5


def rounded(values):
    return values.astype(np.float32).astype(ml_dtypes.bfloat16)


def scan_table(length):
    positions = np.arange(length)
    angles = -2.0 * math.pi / length * (positions[:, None] * positions[None, :] % length)
    factor = 1.0 / math.sqrt(length)
    return rounded(np.cos(angles) * factor), rounded(np.sin(angles) * factor)


def detector_parts(window):
    offsets = np.arange(window)
    phases = (
        offsets[:, None, None, None] * offsets[None, None, :, None]
        + offsets[None, :, None, None] * offsets[None, None, None, :]
    ) % window
    angles = -2.0 * math.pi / window * phases.reshape(window * window, window * window)
    factor = 1.0 / window
    return rounded(np.cos(angles) * factor), rounded(np.sin(angles) * factor)


def y_table(length):
    t_re, t_im = scan_table(length)
    return np.stack([t_re.T, t_im.T], axis=1).reshape(2 * length, length)


def x_table(length, owners, senders, cuts):
    t_re, t_im = scan_table(length)
    upper = np.stack([t_re.T, -t_im.T], axis=1)
    lower = np.stack([t_im.T, t_re.T], axis=1)
    both = np.stack([upper, lower], axis=0)
    width = length // owners
    both = both.reshape(2, owners, width, 2, senders, length // senders).transpose(1, 0, 2, 3, 4, 5)
    parts = [
        both[..., first : first + count].reshape(owners, 2 * width, 2, senders * count)
        for first, count in cuts
    ]
    return np.concatenate(parts, axis=-1).reshape(owners, 2 * width, 2 * length)


def pixel_table(window, depth):
    d_re, d_im = detector_parts(window)
    pixels = window * window
    upper = np.concatenate([d_re, d_im], axis=1).reshape(pixels // depth, depth, 2 * pixels)
    lower = np.concatenate([-d_im, d_re], axis=1).reshape(pixels // depth, depth, 2 * pixels)
    return np.stack([upper, lower], axis=1).reshape(pixels // depth, 2 * depth, 2 * pixels)


def params():
    return pltpu.CompilerParams(vmem_limit_bytes=VMEM_BYTES)


def y_transform(table, pieces, owners, u_chunks):
    n_x, n_y, depth = pieces[0].shape
    per_owner = table.shape[0] // owners
    step = 2

    def body(t_ref, *refs):
        ins, outs = refs[: len(pieces)], refs[len(pieces) :]
        cols = []
        for i in range(step):
            cols.append(jnp.concatenate([p[i] for p in ins], axis=0))
        if depth == LANES:
            rhs = jnp.concatenate(cols, axis=1)
            res = jnp.dot(t_ref[...], rhs, preferred_element_type=jnp.float32)
            parts = [res[:, i * depth : (i + 1) * depth] for i in range(step)]
        else:
            parts = [jnp.dot(t_ref[...], c, preferred_element_type=jnp.float32) for c in cols]
        for i in range(step):
            res = parts[i].astype(jnp.bfloat16)
            for o_ref, (first, count) in zip(outs, u_chunks):
                for d in range(owners):
                    row = d * per_owner + 2 * first
                    o_ref[d, i] = res[row : row + 2 * count]

    out_shape = [
        jax.ShapeDtypeStruct((owners, n_x, 2 * count, depth), jnp.bfloat16) for _, count in u_chunks
    ]
    flops = 2 * table.shape[0] * table.shape[1] * n_x * depth
    moved = 2 * n_x * depth * (table.shape[0] + table.shape[1]) + 2 * table.size
    return pl.pallas_call(
        body,
        grid=(n_x // step,),
        in_specs=[pl.BlockSpec(table.shape, lambda s: (0, 0))]
        + [pl.BlockSpec((step, n_y, depth), lambda s: (s, 0, 0)) for _ in pieces],
        out_specs=[
            pl.BlockSpec((owners, step, 2 * count, depth), lambda s: (0, s, 0, 0))
            for _, count in u_chunks
        ],
        out_shape=out_shape,
        compiler_params=params(),
        cost_estimate=pl.CostEstimate(flops=flops, bytes_accessed=moved, transcendentals=0),
        name="y_transform",
    )(table, *pieces)


def x_transform(table, parts, first, n_u, owners):
    starts = [(first - start) // U_TILE for start, _ in parts]
    parts = [p for _, p in parts]
    depth = parts[0].shape[3]
    v_own = table.shape[0] // owners // 2
    views = [p.reshape(p.shape[0] * p.shape[1], p.shape[2], depth) for p in parts]
    pair = 2

    def body(t_ref, *refs):
        ins, outs = refs[: len(views)], refs[len(views) :]
        turned = [jnp.swapaxes(p[...], 0, 1) for p in ins]
        for u in range(0, U_TILE, pair):
            cols = [
                jnp.concatenate([t[2 * (u + i) + r] for r in range(2) for t in turned], axis=0)
                for i in range(pair)
            ]
            if depth == LANES:
                rhs = jnp.concatenate(cols, axis=1)
                res = jnp.dot(t_ref[...], rhs, preferred_element_type=jnp.float32)
                made = [res[:, i * depth : (i + 1) * depth] for i in range(pair)]
            else:
                made = [jnp.dot(t_ref[...], c, preferred_element_type=jnp.float32) for c in cols]
            for i in range(pair):
                res = made[i].astype(jnp.bfloat16)
                for d in range(owners):
                    for r in range(2):
                        row = (2 * d + r) * v_own
                        outs[d][u + i, r] = res[row : row + v_own]

    flops = 2 * table.size * n_u * depth
    moved = 4 * n_u * depth * table.shape[1] + 2 * table.size

    def placed(view, start):
        return pl.BlockSpec((view.shape[0], 2 * U_TILE, depth), lambda s: (0, start + s, 0))

    return pl.pallas_call(
        body,
        grid=(n_u // U_TILE,),
        in_specs=[pl.BlockSpec(table.shape, lambda s: (0, 0))]
        + [placed(v, start) for v, start in zip(views, starts)],
        out_specs=[
            pl.BlockSpec((U_TILE, 2, v_own, depth), lambda s: (s, 0, 0, 0)) for _ in range(owners)
        ],
        out_shape=[
            jax.ShapeDtypeStruct((n_u, 2, v_own, depth), jnp.bfloat16) for _ in range(owners)
        ],
        compiler_params=params(),
        cost_estimate=pl.CostEstimate(flops=flops, bytes_accessed=moved, transcendentals=0),
        name="x_transform",
    )(table, *views)


def chi_factors(windows, base, table, count_y):
    n_rows, v_own, lanes = windows.shape[1:]
    n_blocks = base.shape[1]
    stride = lanes // WIN
    inner, columns = table.shape
    pixels = columns // 2
    step = min(4, count_y)
    wide = 256

    def body(w_ref, b_ref, t_ref, re_ref, im_ref, left):
        first = pl.program_id(0) * step
        for i in range(step):
            for b in range(n_blocks):
                w_re = w_ref[0, first + i + b * stride]
                w_im = w_ref[1, first + i + b * stride]
                a_re = b_ref[0, b : b + 1]
                a_im = b_ref[1, b : b + 1]
                rows = slice(i * v_own, (i + 1) * v_own)
                at = 2 * b * lanes
                left[rows, at : at + lanes] = (a_re * w_re + a_im * w_im).astype(jnp.bfloat16)
                left[rows, at + lanes : at + 2 * lanes] = (a_im * w_re - a_re * w_im).astype(jnp.bfloat16)
        for n in range(pixels // wide):
            at = slice(n * wide, (n + 1) * wide)
            to = slice(pixels + n * wide, pixels + (n + 1) * wide)
            c_re = jnp.dot(left[...], t_ref[:, at], preferred_element_type=jnp.float32)
            c_im = jnp.dot(left[...], t_ref[:, to], preferred_element_type=jnp.float32)
            scale = 1.0 / (c_re * c_re + c_im * c_im + wiener_floor)
            re_ref[:, :, at] = (c_re * scale).reshape(step, v_own, wide)
            im_ref[:, :, at] = (c_im * scale).reshape(step, v_own, wide)

    rows = count_y * v_own
    return pl.pallas_call(
        body,
        grid=(count_y // step,),
        in_specs=[
            pl.BlockSpec(windows.shape, lambda s: (0, 0, 0, 0)),
            pl.BlockSpec(base.shape, lambda s: (0, 0, 0)),
            pl.BlockSpec(table.shape, lambda s: (0, 0)),
        ],
        out_specs=[pl.BlockSpec((step, v_own, pixels), lambda s: (s, 0, 0))] * 2,
        out_shape=[jax.ShapeDtypeStruct((count_y, v_own, pixels), jnp.float32)] * 2,
        scratch_shapes=[pltpu.VMEM((step * v_own, inner), jnp.bfloat16)],
        compiler_params=params(),
        cost_estimate=pl.CostEstimate(
            flops=2 * rows * table.size, bytes_accessed=2 * table.size + 8 * rows * pixels, transcendentals=0
        ),
        name="chi_factors",
    )(windows, base, table)


def pixel_transform(table, table_rows, pieces, factors, partial, first, count, total_u, previous):
    pixels = table.shape[1] // 2
    arrays = [p for _, p in pieces]
    v_own, depth = arrays[0].shape[2:]
    inner = 2 * depth * len(arrays)
    step = STRIDE_Y
    rows = step * v_own
    lanes = 256
    base = first // step
    block = table_rows // inner

    def body(t_ref, *refs):
        ins, refs = refs[: len(arrays)], refs[len(arrays) :]
        sums, refs = refs[: len(partial)], refs[len(partial) :]
        re_ref, im_ref = refs[-2:]
        cuts = [p[:, r].reshape(rows, depth) for p in ins for r in range(2)]
        if depth == LANES:
            cuts = [jnp.concatenate(cuts, axis=1)]
        size = inner // len(cuts)

        def total(at):
            made = None
            for i, cut in enumerate(cuts):
                term = jnp.dot(cut, t_ref[i * size : (i + 1) * size, at], preferred_element_type=jnp.float32)
                made = term if made is None else made + term
            return made.reshape(step, v_own, lanes)

        for n in range(pixels // lanes):
            at = slice(n * lanes, (n + 1) * lanes)
            s_re = total(at)
            s_im = total(slice(pixels + n * lanes, pixels + (n + 1) * lanes))
            if sums:
                s_re = s_re + sums[0][:, :, at]
                s_im = s_im + sums[1][:, :, at]
            if factors:
                c_re = refs[0][:, :, at]
                c_im = refs[1][:, :, at]
                s_re, s_im = s_re * c_re + s_im * c_im, s_im * c_re - s_re * c_im
            re_ref[:, :, at] = s_re
            im_ref[:, :, at] = s_im

    def placed(start, array):
        return pl.BlockSpec((step, 2, v_own, depth), lambda s: ((first - start) // step + s, 0, 0, 0))

    here = 0 if not factors else base
    shape = jax.ShapeDtypeStruct((total_u if factors else count, v_own, pixels), jnp.float32)
    operands = [table, *arrays, *partial, *factors]
    aliases = {}
    for i, array in enumerate(previous):
        aliases[len(operands)] = i
        operands.append(array)
    return pl.pallas_call(
        body,
        grid=(count // step,),
        in_specs=[pl.BlockSpec((inner, 2 * pixels), lambda s: (block, 0))]
        + [placed(start, p) for start, p in pieces]
        + [pl.BlockSpec((step, v_own, pixels), lambda s: (s, 0, 0)) for _ in partial]
        + [pl.BlockSpec((1, v_own, pixels), lambda s: (base + s, 0, 0)) for _ in factors]
        + [pl.BlockSpec(memory_space=pl.ANY) for _ in previous],
        out_specs=[pl.BlockSpec((step, v_own, pixels), lambda s: (here + s, 0, 0))] * 2,
        out_shape=[shape] * 2,
        input_output_aliases=aliases,
        compiler_params=params(),
        cost_estimate=pl.CostEstimate(
            flops=4 * count * v_own * inner * pixels,
            bytes_accessed=4 * inner * pixels + 12 * count * v_own * pixels,
            transcendentals=0,
        ),
        name="pixel_transform",
    )(*operands)


def signed_shift(freqs, length, step_size):
    centred = jnp.where(freqs >= length // 2, freqs - length, freqs)
    return jnp.floor_divide(centred, step_size)


def probe_windows(probe, shift_y, shift_x, lanes):
    grid_size = probe.shape[-1]
    stride = lanes // WIN
    count_x = shift_x.shape[0]
    n_rows = shift_y.shape[0] + WIN - stride
    rows = (shift_y[0] + jnp.arange(n_rows + stride - 1, dtype=jnp.int32)) % grid_size
    columns = (shift_x[:, None] + jnp.arange(WIN, dtype=jnp.int32)[None, :]) % grid_size
    picked = jnp.take(probe, rows, axis=1, mode="clip")
    chosen = (jnp.arange(grid_size, dtype=jnp.int32)[:, None] == columns.reshape(1, -1)).astype(jnp.float32)
    moved = jnp.einsum("prc,cm->prm", picked, chosen, precision=lax.Precision.HIGHEST)
    moved = moved.reshape(2, n_rows + stride - 1, count_x, WIN)
    return jnp.concatenate([moved[:, p : p + n_rows] for p in range(stride)], axis=-1)


def swap(array, partner, axis):
    size = lax.axis_size(axis)
    return lax.ppermute(array, axis, [(i, i ^ partner) for i in range(size)])


def gather_rows(block, axis):
    rank = lax.axis_index(axis)
    partner = 1
    while partner < lax.axis_size(axis):
        other = swap(block, partner, axis)
        ahead = (rank & partner) > 0
        block = jnp.concatenate(
            [jnp.where(ahead, other, block), jnp.where(ahead, block, other)], axis=1
        )
        partner *= 2
    return block


def shards(frames, probe_wave):
    n_grp, n_mem = lax.axis_size("grp"), lax.axis_size("mem")
    grp, mem = lax.axis_index("grp"), lax.axis_index("mem")
    n_y, n_x, pixels = frames.shape
    scan_y, scan_x = n_y * n_grp, n_x * n_mem
    u_own, v_own = scan_y // n_mem, scan_x // n_grp
    depth = min(LANES, pixels // n_grp)
    n_q = pixels // (n_grp * depth)
    partners = grp ^ jnp.arange(n_grp, dtype=jnp.int32)
    if n_x >= 32:
        opening = 2 * (n_x * 5 // 32)
        x_cuts = [(0, opening), (opening, n_x - opening)]
    else:
        x_cuts = [(0, n_x)]

    if u_own >= 8 * U_TILE:
        sizes = [u_own * 3 // 8, u_own // 4, u_own // 4, u_own // 8]
    else:
        sizes = [u_own // 2, u_own // 2]
    u_chunks = []
    for size in sizes:
        u_chunks.append((sum(c for _, c in u_chunks), size))

    def cut(q, first, count):
        made = []
        for j in range(n_grp - 1, -1, -1):
            at = (q * n_grp + (grp ^ j)) * depth
            piece = lax.dynamic_slice(frames, (0, first, at), (n_y, count, depth))
            made.append(piece.transpose(1, 0, 2))
        return made[::-1]

    def exchange(pieces):
        far = [swap(pieces[j], j, "grp") for j in range(n_grp - 1, 0, -1)]
        return [pieces[0]] + far[::-1]

    def to_owners(array):
        return lax.all_to_all(array, "mem", split_axis=0, concat_axis=0, tiled=True)

    def chosen(table, index, axis):
        return jnp.take(jnp.asarray(table), index, axis=axis, mode="clip")

    ty = chosen(y_table(scan_y).reshape(2 * scan_y, n_grp, n_y), partners, 1)
    ty = ty.reshape(2 * scan_y, scan_y)

    fronts = [(q, first, count) for q in range(n_q - 1) for first, count in x_cuts]
    fronts.append((n_q - 1, 0, n_x))
    halves = [u_chunks[0], (u_chunks[0][1], u_own - u_chunks[0][1])]
    pieces = exchange(cut(*fronts[0]))
    whole_probe = gather_rows(probe_wave, "mem")
    arrived = []
    for i in range(len(fronts) - 1):
        chunks = halves if i == len(fronts) - 2 else [(0, u_own)]
        ready = y_transform(ty, pieces, n_mem, chunks)
        following = cut(*fronts[i + 1])
        ready, following, whole_probe, arrived = lax.optimization_barrier(
            (ready, following, whole_probe, arrived)
        )
        arrived.append(to_owners(ready[0]))
        pieces = exchange(following)

    shift_y = signed_shift(
        mem * u_own + STRIDE_Y * jnp.arange(u_own // STRIDE_Y, dtype=jnp.int32), scan_y, STRIDE_Y
    )
    shift_x = signed_shift(grp * v_own + jnp.arange(v_own, dtype=jnp.int32), scan_x, STRIDE_X)
    base = whole_probe[:, :WIN, :WIN].reshape(2, WIN * WIN // LANES, LANES)
    windows = probe_windows(whole_probe, shift_y, shift_x, LANES)
    chi_table = jnp.asarray(pixel_table(WIN, LANES).reshape(2 * pixels, 2 * pixels))
    factors = chi_factors(windows, base, chi_table, u_own // STRIDE_Y)
    tx, tx_late = (
        chosen(x_table(scan_x, n_grp, n_mem, cuts), partners, 0).reshape(2 * scan_x, 2 * scan_x)
        for cuts in (x_cuts, [(0, n_x)])
    )
    blocks = (jnp.arange(n_q, dtype=jnp.int32)[:, None] * n_grp + partners[None, :]).reshape(-1)
    tk = chosen(pixel_table(WIN, depth), blocks, 0).reshape(2 * pixels, 2 * pixels)

    early = []
    late = []
    if fronts[:-1]:
        arrived, pending, factors, tx, pieces = lax.optimization_barrier((arrived, ready[1], factors, tx, pieces))
        last = to_owners(pending)
        late_ready = y_transform(ty, pieces, n_mem, u_chunks)
        sources = [(0, a) for a in arrived]
        early.append(exchange(x_transform(tx, sources, *halves[0], n_grp)))
        late_ready, last, tk, tx_late, early[0] = lax.optimization_barrier(
            (late_ready, last, tk, tx_late, early[0])
        )
        sources = sources[:-1] + [(halves[1][0], last)]
        last = to_owners(late_ready[0])
        early.append(exchange(x_transform(tx, sources, *halves[1], n_grp)))
    else:
        late_ready = y_transform(ty, pieces, n_mem, u_chunks)
        last = to_owners(late_ready[0])

    def early_of(first):
        return [(start, p) for (start, size), part in zip(halves, early) if start <= first < start + size for p in part]

    inner = 2 * pixels // n_q
    def finish(c, outs):
        first, count = u_chunks[c]
        own = [(first, p) for p in late[c]]
        if c == len(u_chunks) - 1 and partial:
            return pixel_transform(tk, inner, own, factors, partial, first, count, u_own, outs)
        return pixel_transform(tk, 0, early_of(first) + own, factors, [], first, count, u_own, outs)

    outs = []
    partial = []
    for c in range(1, len(u_chunks)):
        sending, last, early, late, partial, outs = lax.optimization_barrier(
            (late_ready[c], last, early, late, partial, outs)
        )
        following = to_owners(sending)
        first, count = u_chunks[c - 1]
        late.append(exchange(x_transform(tx_late, [(first, last)], first, count, n_grp)))
        last = following
        if c == 1 and early:
            first, count = u_chunks[-1]
            partial = pixel_transform(tk, 0, early_of(first), [], [], first, count, u_own, [])
        if c >= 2:
            outs = finish(c - 2, outs)
    last, partial, outs = lax.optimization_barrier((last, partial, outs))
    first, count = u_chunks[-1]
    late.append(exchange(x_transform(tx_late, [(first, last)], first, count, n_grp)))
    for c in range(max(0, len(u_chunks) - 2), len(u_chunks)):
        outs = finish(c, outs)
    return tuple(outs)


def solution(mesh):
    return jax.shard_map(
        shards,
        mesh=mesh,
        in_specs=(P("grp", "mem", None), P(None, "mem", None)),
        out_specs=(P("mem", "grp", None), P("mem", "grp", None)),
        check_vma=False,
    )
```

```python
import math

import jax
import jax.numpy as jnp
import numpy as np
from jax import lax
from jax.experimental import pallas as pl
from jax.experimental.pallas import tpu as pltpu
from jax.sharding import PartitionSpec as P
import ml_dtypes

WIN = 32
STRIDE_Y = 4
STRIDE_X = 2
LANES = 128
U_TILE = 8
VMEM_BYTES = 36 * 1024 * 1024
LARGE_VMEM_BYTES = 56 * 1024 * 1024

wiener_floor = 0.5


def rounded(values):
    return values.astype(np.float32).astype(ml_dtypes.bfloat16)


def scan_table(length):
    positions = np.arange(length)
    angles = -2.0 * math.pi / length * (positions[:, None] * positions[None, :] % length)
    factor = 1.0 / math.sqrt(length)
    return rounded(np.cos(angles) * factor), rounded(np.sin(angles) * factor)


def detector_parts(window):
    offsets = np.arange(window)
    phases = (
        offsets[:, None, None, None] * offsets[None, None, :, None]
        + offsets[None, :, None, None] * offsets[None, None, None, :]
    ) % window
    angles = -2.0 * math.pi / window * phases.reshape(window * window, window * window)
    factor = 1.0 / window
    return rounded(np.cos(angles) * factor), rounded(np.sin(angles) * factor)


def y_table(length):
    t_re, t_im = scan_table(length)
    return np.stack([t_re.T, t_im.T], axis=1).reshape(2 * length, length)


def x_table(length, owners, senders, cuts):
    t_re, t_im = scan_table(length)
    upper = np.stack([t_re.T, -t_im.T], axis=1)
    lower = np.stack([t_im.T, t_re.T], axis=1)
    both = np.stack([upper, lower], axis=0)
    width = length // owners
    both = both.reshape(2, owners, width, 2, senders, length // senders).transpose(1, 0, 2, 3, 4, 5)
    parts = [
        both[..., first : first + count].reshape(owners, 2 * width, 2, senders * count)
        for first, count in cuts
    ]
    return np.concatenate(parts, axis=-1).reshape(owners, 2 * width, 2 * length)


def pixel_table(window, depth):
    d_re, d_im = detector_parts(window)
    pixels = window * window
    upper = np.concatenate([d_re, d_im], axis=1).reshape(pixels // depth, depth, 2 * pixels)
    lower = np.concatenate([-d_im, d_re], axis=1).reshape(pixels // depth, depth, 2 * pixels)
    return np.stack([upper, lower], axis=1).reshape(pixels // depth, 2 * depth, 2 * pixels)


def params(limit=VMEM_BYTES):
    return pltpu.CompilerParams(vmem_limit_bytes=limit)


def y_transform(table, pieces, owners, u_chunks):
    n_x, n_y, depth = pieces[0].shape
    per_owner = table.shape[0] // owners
    step = 2

    def body(t_ref, *refs):
        ins, outs = refs[: len(pieces)], refs[len(pieces) :]
        cols = []
        for i in range(step):
            cols.append(jnp.concatenate([p[i] for p in ins], axis=0))
        if depth == LANES:
            rhs = jnp.concatenate(cols, axis=1)
            res = jnp.dot(t_ref[...], rhs, preferred_element_type=jnp.float32)
            parts = [res[:, i * depth : (i + 1) * depth] for i in range(step)]
        else:
            parts = [jnp.dot(t_ref[...], c, preferred_element_type=jnp.float32) for c in cols]
        for i in range(step):
            res = parts[i].astype(jnp.bfloat16)
            for o_ref, (first, count) in zip(outs, u_chunks):
                for d in range(owners):
                    row = d * per_owner + 2 * first
                    o_ref[d, i] = res[row : row + 2 * count]

    out_shape = [
        jax.ShapeDtypeStruct((owners, n_x, 2 * count, depth), jnp.bfloat16) for _, count in u_chunks
    ]
    flops = 2 * table.shape[0] * table.shape[1] * n_x * depth
    moved = 2 * n_x * depth * (table.shape[0] + table.shape[1]) + 2 * table.size
    return pl.pallas_call(
        body,
        grid=(n_x // step,),
        in_specs=[pl.BlockSpec(table.shape, lambda s: (0, 0))]
        + [pl.BlockSpec((step, n_y, depth), lambda s: (s, 0, 0)) for _ in pieces],
        out_specs=[
            pl.BlockSpec((owners, step, 2 * count, depth), lambda s: (0, s, 0, 0))
            for _, count in u_chunks
        ],
        out_shape=out_shape,
        compiler_params=params(),
        cost_estimate=pl.CostEstimate(flops=flops, bytes_accessed=moved, transcendentals=0),
        name="y_transform",
    )(table, *pieces)


def x_transform(table, parts, first, n_u, owners):
    starts = [(first - start) // U_TILE for start, _ in parts]
    parts = [p for _, p in parts]
    depth = parts[0].shape[3]
    v_own = table.shape[0] // owners // 2
    views = [p.reshape(p.shape[0] * p.shape[1], p.shape[2], depth) for p in parts]
    pair = 2

    def body(t_ref, *refs):
        ins, outs = refs[: len(views)], refs[len(views) :]
        turned = [jnp.swapaxes(p[...], 0, 1) for p in ins]
        for u in range(0, U_TILE, pair):
            cols = [
                jnp.concatenate([t[2 * (u + i) + r] for r in range(2) for t in turned], axis=0)
                for i in range(pair)
            ]
            if depth == LANES:
                rhs = jnp.concatenate(cols, axis=1)
                res = jnp.dot(t_ref[...], rhs, preferred_element_type=jnp.float32)
                made = [res[:, i * depth : (i + 1) * depth] for i in range(pair)]
            else:
                made = [jnp.dot(t_ref[...], c, preferred_element_type=jnp.float32) for c in cols]
            for i in range(pair):
                res = made[i].astype(jnp.bfloat16)
                for d in range(owners):
                    for r in range(2):
                        row = (2 * d + r) * v_own
                        outs[d][u + i, r] = res[row : row + v_own]

    flops = 2 * table.size * n_u * depth
    moved = 4 * n_u * depth * table.shape[1] + 2 * table.size

    def placed(view, start):
        return pl.BlockSpec((view.shape[0], 2 * U_TILE, depth), lambda s: (0, start + s, 0))

    return pl.pallas_call(
        body,
        grid=(n_u // U_TILE,),
        in_specs=[pl.BlockSpec(table.shape, lambda s: (0, 0))]
        + [placed(v, start) for v, start in zip(views, starts)],
        out_specs=[
            pl.BlockSpec((U_TILE, 2, v_own, depth), lambda s: (s, 0, 0, 0)) for _ in range(owners)
        ],
        out_shape=[
            jax.ShapeDtypeStruct((n_u, 2, v_own, depth), jnp.bfloat16) for _ in range(owners)
        ],
        compiler_params=params(),
        cost_estimate=pl.CostEstimate(flops=flops, bytes_accessed=moved, transcendentals=0),
        name="x_transform",
    )(table, *views)


def chi_factors(windows, base, table, count_y):
    n_rows, v_own, lanes = windows.shape[1:]
    n_blocks = base.shape[1]
    stride = lanes // WIN
    inner, columns = table.shape
    pixels = columns // 2
    step = min(4, count_y)
    wide = 256

    def body(w_ref, b_ref, t_ref, re_ref, im_ref, left):
        first = pl.program_id(0) * step
        for i in range(step):
            for b in range(n_blocks):
                w_re = w_ref[0, first + i + b * stride]
                w_im = w_ref[1, first + i + b * stride]
                a_re = b_ref[0, b : b + 1]
                a_im = b_ref[1, b : b + 1]
                rows = slice(i * v_own, (i + 1) * v_own)
                at = 2 * b * lanes
                left[rows, at : at + lanes] = (a_re * w_re + a_im * w_im).astype(jnp.bfloat16)
                left[rows, at + lanes : at + 2 * lanes] = (a_im * w_re - a_re * w_im).astype(jnp.bfloat16)
        for n in range(pixels // wide):
            at = slice(n * wide, (n + 1) * wide)
            to = slice(pixels + n * wide, pixels + (n + 1) * wide)
            c_re = jnp.dot(left[...], t_ref[:, at], preferred_element_type=jnp.float32)
            c_im = jnp.dot(left[...], t_ref[:, to], preferred_element_type=jnp.float32)
            scale = 1.0 / (c_re * c_re + c_im * c_im + wiener_floor)
            re_ref[:, :, at] = (c_re * scale).reshape(step, v_own, wide)
            im_ref[:, :, at] = (c_im * scale).reshape(step, v_own, wide)

    rows = count_y * v_own
    return pl.pallas_call(
        body,
        grid=(count_y // step,),
        in_specs=[
            pl.BlockSpec(windows.shape, lambda s: (0, 0, 0, 0)),
            pl.BlockSpec(base.shape, lambda s: (0, 0, 0)),
            pl.BlockSpec(table.shape, lambda s: (0, 0)),
        ],
        out_specs=[pl.BlockSpec((step, v_own, pixels), lambda s: (s, 0, 0))] * 2,
        out_shape=[jax.ShapeDtypeStruct((count_y, v_own, pixels), jnp.float32)] * 2,
        scratch_shapes=[pltpu.VMEM((step * v_own, inner), jnp.bfloat16)],
        compiler_params=params(),
        cost_estimate=pl.CostEstimate(
            flops=2 * rows * table.size, bytes_accessed=2 * table.size + 8 * rows * pixels, transcendentals=0
        ),
        name="chi_factors",
    )(windows, base, table)


def pixel_transform(table, table_rows, pieces, factors, partial, first, count, total_u, previous):
    pixels = table.shape[1] // 2
    arrays = [p for _, p in pieces]
    v_own, depth = arrays[0].shape[2:]
    inner = 2 * depth * len(arrays)
    step = STRIDE_Y
    rows = step * v_own
    lanes = 256
    base = first // step
    block = table_rows // inner

    def body(t_ref, *refs):
        ins, refs = refs[: len(arrays)], refs[len(arrays) :]
        sums, refs = refs[: len(partial)], refs[len(partial) :]
        re_ref, im_ref = refs[-2:]
        cuts = [p[:, r].reshape(rows, depth) for p in ins for r in range(2)]
        if depth == LANES:
            cuts = [jnp.concatenate(cuts, axis=1)]
        size = inner // len(cuts)

        def total(at):
            made = None
            for i, cut in enumerate(cuts):
                term = jnp.dot(cut, t_ref[i * size : (i + 1) * size, at], preferred_element_type=jnp.float32)
                made = term if made is None else made + term
            return made.reshape(step, v_own, lanes)

        for n in range(pixels // lanes):
            at = slice(n * lanes, (n + 1) * lanes)
            s_re = total(at)
            s_im = total(slice(pixels + n * lanes, pixels + (n + 1) * lanes))
            if sums:
                s_re = s_re + sums[0][:, :, at]
                s_im = s_im + sums[1][:, :, at]
            if factors:
                c_re = refs[0][:, :, at]
                c_im = refs[1][:, :, at]
                s_re, s_im = s_re * c_re + s_im * c_im, s_im * c_re - s_re * c_im
            re_ref[:, :, at] = s_re
            im_ref[:, :, at] = s_im

    def placed(start, array):
        return pl.BlockSpec((step, 2, v_own, depth), lambda s: ((first - start) // step + s, 0, 0, 0))

    here = 0 if not factors else base
    shape = jax.ShapeDtypeStruct((total_u if factors else count, v_own, pixels), jnp.float32)
    operands = [table, *arrays, *partial, *factors]
    aliases = {}
    for i, array in enumerate(previous):
        aliases[len(operands)] = i
        operands.append(array)
    return pl.pallas_call(
        body,
        grid=(count // step,),
        in_specs=[pl.BlockSpec((inner, 2 * pixels), lambda s: (block, 0))]
        + [placed(start, p) for start, p in pieces]
        + [pl.BlockSpec((step, v_own, pixels), lambda s: (s, 0, 0)) for _ in partial]
        + [pl.BlockSpec((1, v_own, pixels), lambda s: (base + s, 0, 0)) for _ in factors]
        + [pl.BlockSpec(memory_space=pl.ANY) for _ in previous],
        out_specs=[pl.BlockSpec((step, v_own, pixels), lambda s: (here + s, 0, 0))] * 2,
        out_shape=[shape] * 2,
        input_output_aliases=aliases,
        compiler_params=params(LARGE_VMEM_BYTES),
        cost_estimate=pl.CostEstimate(
            flops=4 * count * v_own * inner * pixels,
            bytes_accessed=4 * inner * pixels + 12 * count * v_own * pixels,
            transcendentals=0,
        ),
        name="pixel_transform",
    )(*operands)


def signed_shift(freqs, length, step_size):
    centred = jnp.where(freqs >= length // 2, freqs - length, freqs)
    return jnp.floor_divide(centred, step_size)


def probe_windows(probe, shift_y, shift_x, lanes):
    grid_size = probe.shape[-1]
    stride = lanes // WIN
    count_x = shift_x.shape[0]
    n_rows = shift_y.shape[0] + WIN - stride
    rows = (shift_y[0] + jnp.arange(n_rows + stride - 1, dtype=jnp.int32)) % grid_size
    columns = (shift_x[:, None] + jnp.arange(WIN, dtype=jnp.int32)[None, :]) % grid_size
    picked = jnp.take(probe, rows, axis=1, mode="clip")
    chosen = (jnp.arange(grid_size, dtype=jnp.int32)[:, None] == columns.reshape(1, -1)).astype(jnp.float32)
    moved = jnp.einsum("prc,cm->prm", picked, chosen, precision=lax.Precision.HIGHEST)
    moved = moved.reshape(2, n_rows + stride - 1, count_x, WIN)
    return jnp.concatenate([moved[:, p : p + n_rows] for p in range(stride)], axis=-1)


def swap(array, partner, axis):
    size = lax.axis_size(axis)
    return lax.ppermute(array, axis, [(i, i ^ partner) for i in range(size)])


def gather_rows(block, axis):
    rank = lax.axis_index(axis)
    partner = 1
    while partner < lax.axis_size(axis):
        other = swap(block, partner, axis)
        ahead = (rank & partner) > 0
        block = jnp.concatenate(
            [jnp.where(ahead, other, block), jnp.where(ahead, block, other)], axis=1
        )
        partner *= 2
    return block


def shards(frames, probe_wave):
    n_grp, n_mem = lax.axis_size("grp"), lax.axis_size("mem")
    grp, mem = lax.axis_index("grp"), lax.axis_index("mem")
    n_y, n_x, pixels = frames.shape
    scan_y, scan_x = n_y * n_grp, n_x * n_mem
    u_own, v_own = scan_y // n_mem, scan_x // n_grp
    depth = min(LANES, pixels // n_grp)
    n_q = pixels // (n_grp * depth)
    partners = grp ^ jnp.arange(n_grp, dtype=jnp.int32)
    if n_x >= 32:
        opening = n_x // 4
        x_cuts = [(0, opening), (opening, n_x - opening)]
    else:
        x_cuts = [(0, n_x)]

    if u_own >= 8 * U_TILE:
        sizes = [u_own * 3 // 8, u_own // 4, u_own // 4, u_own // 8]
    else:
        sizes = [u_own // 2, u_own // 2]
    u_chunks = []
    for size in sizes:
        u_chunks.append((sum(c for _, c in u_chunks), size))

    def cut(q, first, count):
        made = []
        for j in range(n_grp - 1, -1, -1):
            at = (q * n_grp + (grp ^ j)) * depth
            piece = lax.dynamic_slice(frames, (0, first, at), (n_y, count, depth))
            made.append(piece.transpose(1, 0, 2))
        return made[::-1]

    def exchange(pieces):
        far = [swap(pieces[j], j, "grp") for j in range(n_grp - 1, 0, -1)]
        return [pieces[0]] + far[::-1]

    def to_owners(array):
        return lax.all_to_all(array, "mem", split_axis=0, concat_axis=0, tiled=True)

    def chosen(table, index, axis):
        return jnp.take(jnp.asarray(table), index, axis=axis, mode="clip")

    ty = chosen(y_table(scan_y).reshape(2 * scan_y, n_grp, n_y), partners, 1)
    ty = ty.reshape(2 * scan_y, scan_y)

    fronts = [(q, first, count) for q in range(n_q - 1) for first, count in x_cuts]
    fronts.append((n_q - 1, 0, n_x))
    halves = [u_chunks[0], (u_chunks[0][1], u_own - u_chunks[0][1])]
    pieces = cut(*fronts[0])
    pieces[n_grp // 2 :], probe_wave = lax.optimization_barrier((pieces[n_grp // 2 :], probe_wave))
    pieces = exchange(pieces)
    whole_probe = gather_rows(probe_wave, "mem")
    arrived = []
    for i in range(len(fronts) - 1):
        chunks = halves if i == len(fronts) - 2 else [(0, u_own)]
        ready = y_transform(ty, pieces, n_mem, chunks)
        following = cut(*fronts[i + 1])
        ready, following, whole_probe, arrived = lax.optimization_barrier(
            (ready, following, whole_probe, arrived)
        )
        arrived.append(to_owners(ready[0]))
        pieces = exchange(following)

    shift_y = signed_shift(
        mem * u_own + STRIDE_Y * jnp.arange(u_own // STRIDE_Y, dtype=jnp.int32), scan_y, STRIDE_Y
    )
    shift_x = signed_shift(grp * v_own + jnp.arange(v_own, dtype=jnp.int32), scan_x, STRIDE_X)
    base = whole_probe[:, :WIN, :WIN].reshape(2, WIN * WIN // LANES, LANES)
    windows = probe_windows(whole_probe, shift_y, shift_x, LANES)
    chi_table = jnp.asarray(pixel_table(WIN, LANES).reshape(2 * pixels, 2 * pixels))
    factors = chi_factors(windows, base, chi_table, u_own // STRIDE_Y)
    tx, tx_late = (
        chosen(x_table(scan_x, n_grp, n_mem, cuts), partners, 0).reshape(2 * scan_x, 2 * scan_x)
        for cuts in (x_cuts, [(0, n_x)])
    )
    blocks = (jnp.arange(n_q, dtype=jnp.int32)[:, None] * n_grp + partners[None, :]).reshape(-1)
    tk = chosen(pixel_table(WIN, depth), blocks, 0).reshape(2 * pixels, 2 * pixels)

    early = []
    late = []
    if fronts[:-1]:
        arrived, pending, factors, tx, pieces = lax.optimization_barrier((arrived, ready[1], factors, tx, pieces))
        last = to_owners(pending)
        late_ready = y_transform(ty, pieces, n_mem, u_chunks)
        sources = [(0, a) for a in arrived]
        early.append(exchange(x_transform(tx, sources, *halves[0], n_grp)))
        late_ready, last, tk, tx_late, early[0] = lax.optimization_barrier(
            (late_ready, last, tk, tx_late, early[0])
        )
        sources = sources[:-1] + [(halves[1][0], last)]
        last = to_owners(late_ready[0])
        early.append(exchange(x_transform(tx, sources, *halves[1], n_grp)))
    else:
        late_ready = y_transform(ty, pieces, n_mem, u_chunks)
        last = to_owners(late_ready[0])

    def early_of(first):
        return [(start, p) for (start, size), part in zip(halves, early) if start <= first < start + size for p in part]

    inner = 2 * pixels // n_q
    def finish(c, outs):
        first, count = u_chunks[c]
        own = [(first, p) for p in late[c]]
        if partials[c]:
            return pixel_transform(tk, inner, own, factors, partials[c], first, count, u_own, outs)
        return pixel_transform(tk, 0, early_of(first) + own, factors, [], first, count, u_own, outs)

    outs = []
    partials = [[] for _ in u_chunks]
    for c in range(1, len(u_chunks)):
        sending, last, early, late, partials, outs = lax.optimization_barrier(
            (late_ready[c], last, early, late, partials, outs)
        )
        following = to_owners(sending)
        first, count = u_chunks[c - 1]
        late.append(exchange(x_transform(tx_late, [(first, last)], first, count, n_grp)))
        last = following
        if c == 1 and early:
            for later in range(len(u_chunks) - 2, len(u_chunks)):
                first, count = u_chunks[later]
                partials[later] = pixel_transform(tk, 0, early_of(first), [], [], first, count, u_own, [])
        if c >= 2:
            outs = finish(c - 2, outs)
    last, partials, outs = lax.optimization_barrier((last, partials, outs))
    first, count = u_chunks[-1]
    late.append(exchange(x_transform(tx_late, [(first, last)], first, count, n_grp)))
    for c in range(max(0, len(u_chunks) - 2), len(u_chunks)):
        outs = finish(c, outs)
    return tuple(outs)


def solution(mesh):
    return jax.shard_map(
        shards,
        mesh=mesh,
        in_specs=(P("grp", "mem", None), P(None, "mem", None)),
        out_specs=(P("mem", "grp", None), P("mem", "grp", None)),
        check_vma=False,
    )
```

```python
import math

import jax
import jax.numpy as jnp
import numpy as np
from jax import lax
from jax.experimental import pallas as pl
from jax.experimental.pallas import tpu as pltpu
from jax.sharding import PartitionSpec as P
import ml_dtypes

WIN = 32
STRIDE_Y = 4
STRIDE_X = 2
LANES = 128
U_TILE = 8
VMEM_BYTES = 36 * 1024 * 1024
LARGE_VMEM_BYTES = 56 * 1024 * 1024

wiener_floor = 0.5


def rounded(values):
    return values.astype(np.float32).astype(ml_dtypes.bfloat16)


def scan_table(length):
    positions = np.arange(length)
    angles = -2.0 * math.pi / length * (positions[:, None] * positions[None, :] % length)
    factor = 1.0 / math.sqrt(length)
    return rounded(np.cos(angles) * factor), rounded(np.sin(angles) * factor)


def detector_parts(window):
    offsets = np.arange(window)
    phases = (
        offsets[:, None, None, None] * offsets[None, None, :, None]
        + offsets[None, :, None, None] * offsets[None, None, None, :]
    ) % window
    angles = -2.0 * math.pi / window * phases.reshape(window * window, window * window)
    factor = 1.0 / window
    return rounded(np.cos(angles) * factor), rounded(np.sin(angles) * factor)


def y_table(length):
    t_re, t_im = scan_table(length)
    return np.stack([t_re.T, t_im.T], axis=1).reshape(2 * length, length)


def x_table(length, owners, senders, cuts):
    t_re, t_im = scan_table(length)
    upper = np.stack([t_re.T, -t_im.T], axis=1)
    lower = np.stack([t_im.T, t_re.T], axis=1)
    both = np.stack([upper, lower], axis=0)
    width = length // owners
    both = both.reshape(2, owners, width, 2, senders, length // senders).transpose(1, 0, 2, 3, 4, 5)
    parts = [
        both[..., first : first + count].reshape(owners, 2 * width, 2, senders * count)
        for first, count in cuts
    ]
    return np.concatenate(parts, axis=-1).reshape(owners, 2 * width, 2 * length)


def pixel_table(window, depth):
    d_re, d_im = detector_parts(window)
    pixels = window * window
    upper = np.concatenate([d_re, d_im], axis=1).reshape(pixels // depth, depth, 2 * pixels)
    lower = np.concatenate([-d_im, d_re], axis=1).reshape(pixels // depth, depth, 2 * pixels)
    return np.stack([upper, lower], axis=1).reshape(pixels // depth, 2 * depth, 2 * pixels)


def params(limit=VMEM_BYTES):
    return pltpu.CompilerParams(vmem_limit_bytes=limit)


def y_transform(table, pieces, owners, u_chunks):
    n_x, n_y, depth = pieces[0].shape
    per_owner = table.shape[0] // owners
    step = 2

    def body(t_ref, *refs):
        ins, outs = refs[: len(pieces)], refs[len(pieces) :]
        cols = []
        for i in range(step):
            cols.append(jnp.concatenate([p[i] for p in ins], axis=0))
        if depth == LANES:
            rhs = jnp.concatenate(cols, axis=1)
            res = jnp.dot(t_ref[...], rhs, preferred_element_type=jnp.float32)
            parts = [res[:, i * depth : (i + 1) * depth] for i in range(step)]
        else:
            parts = [jnp.dot(t_ref[...], c, preferred_element_type=jnp.float32) for c in cols]
        for i in range(step):
            res = parts[i].astype(jnp.bfloat16)
            for o_ref, (first, count) in zip(outs, u_chunks):
                for d in range(owners):
                    row = d * per_owner + 2 * first
                    o_ref[d, i] = res[row : row + 2 * count]

    out_shape = [
        jax.ShapeDtypeStruct((owners, n_x, 2 * count, depth), jnp.bfloat16) for _, count in u_chunks
    ]
    flops = 2 * table.shape[0] * table.shape[1] * n_x * depth
    moved = 2 * n_x * depth * (table.shape[0] + table.shape[1]) + 2 * table.size
    return pl.pallas_call(
        body,
        grid=(n_x // step,),
        in_specs=[pl.BlockSpec(table.shape, lambda s: (0, 0))]
        + [pl.BlockSpec((step, n_y, depth), lambda s: (s, 0, 0)) for _ in pieces],
        out_specs=[
            pl.BlockSpec((owners, step, 2 * count, depth), lambda s: (0, s, 0, 0))
            for _, count in u_chunks
        ],
        out_shape=out_shape,
        compiler_params=params(),
        cost_estimate=pl.CostEstimate(flops=flops, bytes_accessed=moved, transcendentals=0),
        name="y_transform",
    )(table, *pieces)


def x_transform(table, parts, first, n_u, owners):
    starts = [(first - start) // U_TILE for start, _ in parts]
    parts = [p for _, p in parts]
    depth = parts[0].shape[3]
    v_own = table.shape[0] // owners // 2
    views = [p.reshape(p.shape[0] * p.shape[1], p.shape[2], depth) for p in parts]
    pair = 2

    def body(t_ref, *refs):
        ins, outs = refs[: len(views)], refs[len(views) :]
        turned = [jnp.swapaxes(p[...], 0, 1) for p in ins]
        for u in range(0, U_TILE, pair):
            cols = [
                jnp.concatenate([t[2 * (u + i) + r] for r in range(2) for t in turned], axis=0)
                for i in range(pair)
            ]
            if depth == LANES:
                rhs = jnp.concatenate(cols, axis=1)
                res = jnp.dot(t_ref[...], rhs, preferred_element_type=jnp.float32)
                made = [res[:, i * depth : (i + 1) * depth] for i in range(pair)]
            else:
                made = [jnp.dot(t_ref[...], c, preferred_element_type=jnp.float32) for c in cols]
            for i in range(pair):
                res = made[i].astype(jnp.bfloat16)
                for d in range(owners):
                    for r in range(2):
                        row = (2 * d + r) * v_own
                        outs[d][u + i, r] = res[row : row + v_own]

    flops = 2 * table.size * n_u * depth
    moved = 4 * n_u * depth * table.shape[1] + 2 * table.size

    def placed(view, start):
        return pl.BlockSpec((view.shape[0], 2 * U_TILE, depth), lambda s: (0, start + s, 0))

    return pl.pallas_call(
        body,
        grid=(n_u // U_TILE,),
        in_specs=[pl.BlockSpec(table.shape, lambda s: (0, 0))]
        + [placed(v, start) for v, start in zip(views, starts)],
        out_specs=[
            pl.BlockSpec((U_TILE, 2, v_own, depth), lambda s: (s, 0, 0, 0)) for _ in range(owners)
        ],
        out_shape=[
            jax.ShapeDtypeStruct((n_u, 2, v_own, depth), jnp.bfloat16) for _ in range(owners)
        ],
        compiler_params=params(),
        cost_estimate=pl.CostEstimate(flops=flops, bytes_accessed=moved, transcendentals=0),
        name="x_transform",
    )(table, *views)


def chi_factors(windows, base, table, count_y):
    n_rows, v_own, lanes = windows.shape[1:]
    n_blocks = base.shape[1]
    stride = lanes // WIN
    inner, columns = table.shape
    pixels = columns // 2
    step = min(4, count_y)
    wide = 256

    def body(w_ref, b_ref, t_ref, re_ref, im_ref, left):
        first = pl.program_id(0) * step
        for i in range(step):
            for b in range(n_blocks):
                w_re = w_ref[0, first + i + b * stride]
                w_im = w_ref[1, first + i + b * stride]
                a_re = b_ref[0, b : b + 1]
                a_im = b_ref[1, b : b + 1]
                rows = slice(i * v_own, (i + 1) * v_own)
                at = 2 * b * lanes
                left[rows, at : at + lanes] = (a_re * w_re + a_im * w_im).astype(jnp.bfloat16)
                left[rows, at + lanes : at + 2 * lanes] = (a_im * w_re - a_re * w_im).astype(jnp.bfloat16)
        for n in range(pixels // wide):
            at = slice(n * wide, (n + 1) * wide)
            to = slice(pixels + n * wide, pixels + (n + 1) * wide)
            c_re = jnp.dot(left[...], t_ref[:, at], preferred_element_type=jnp.float32)
            c_im = jnp.dot(left[...], t_ref[:, to], preferred_element_type=jnp.float32)
            scale = 1.0 / (c_re * c_re + c_im * c_im + wiener_floor)
            re_ref[:, :, at] = (c_re * scale).reshape(step, v_own, wide)
            im_ref[:, :, at] = (c_im * scale).reshape(step, v_own, wide)

    rows = count_y * v_own
    return pl.pallas_call(
        body,
        grid=(count_y // step,),
        in_specs=[
            pl.BlockSpec(windows.shape, lambda s: (0, 0, 0, 0)),
            pl.BlockSpec(base.shape, lambda s: (0, 0, 0)),
            pl.BlockSpec(table.shape, lambda s: (0, 0)),
        ],
        out_specs=[pl.BlockSpec((step, v_own, pixels), lambda s: (s, 0, 0))] * 2,
        out_shape=[jax.ShapeDtypeStruct((count_y, v_own, pixels), jnp.float32)] * 2,
        scratch_shapes=[pltpu.VMEM((step * v_own, inner), jnp.bfloat16)],
        compiler_params=params(),
        cost_estimate=pl.CostEstimate(
            flops=2 * rows * table.size, bytes_accessed=2 * table.size + 8 * rows * pixels, transcendentals=0
        ),
        name="chi_factors",
    )(windows, base, table)


def pixel_transform(table, table_rows, pieces, factors, partial, first, count, total_u, previous):
    pixels = table.shape[1] // 2
    arrays = [p for _, p in pieces]
    v_own, depth = arrays[0].shape[2:]
    inner = 2 * depth * len(arrays)
    step = STRIDE_Y
    rows = step * v_own
    lanes = 256
    base = first // step
    block = table_rows // inner

    def body(t_ref, *refs):
        ins, refs = refs[: len(arrays)], refs[len(arrays) :]
        sums, refs = refs[: len(partial)], refs[len(partial) :]
        re_ref, im_ref = refs[-2:]
        cuts = [p[:, r].reshape(rows, depth) for p in ins for r in range(2)]
        if depth == LANES:
            cuts = [jnp.concatenate(cuts, axis=1)]
        size = inner // len(cuts)

        def total(at):
            made = None
            for i, cut in enumerate(cuts):
                term = jnp.dot(cut, t_ref[i * size : (i + 1) * size, at], preferred_element_type=jnp.float32)
                made = term if made is None else made + term
            return made.reshape(step, v_own, lanes)

        for n in range(pixels // lanes):
            at = slice(n * lanes, (n + 1) * lanes)
            s_re = total(at)
            s_im = total(slice(pixels + n * lanes, pixels + (n + 1) * lanes))
            if sums:
                s_re = s_re + sums[0][:, :, at]
                s_im = s_im + sums[1][:, :, at]
            if factors:
                c_re = refs[0][:, :, at]
                c_im = refs[1][:, :, at]
                s_re, s_im = s_re * c_re + s_im * c_im, s_im * c_re - s_re * c_im
            re_ref[:, :, at] = s_re
            im_ref[:, :, at] = s_im

    def placed(start, array):
        return pl.BlockSpec((step, 2, v_own, depth), lambda s: ((first - start) // step + s, 0, 0, 0))

    here = 0 if not factors else base
    shape = jax.ShapeDtypeStruct((total_u if factors else count, v_own, pixels), jnp.float32)
    operands = [table, *arrays, *partial, *factors]
    aliases = {}
    for i, array in enumerate(previous):
        aliases[len(operands)] = i
        operands.append(array)
    return pl.pallas_call(
        body,
        grid=(count // step,),
        in_specs=[pl.BlockSpec((inner, 2 * pixels), lambda s: (block, 0))]
        + [placed(start, p) for start, p in pieces]
        + [pl.BlockSpec((step, v_own, pixels), lambda s: (s, 0, 0)) for _ in partial]
        + [pl.BlockSpec((1, v_own, pixels), lambda s: (base + s, 0, 0)) for _ in factors]
        + [pl.BlockSpec(memory_space=pl.ANY) for _ in previous],
        out_specs=[pl.BlockSpec((step, v_own, pixels), lambda s: (here + s, 0, 0))] * 2,
        out_shape=[shape] * 2,
        input_output_aliases=aliases,
        compiler_params=params(VMEM_BYTES if factors and first + count == total_u else LARGE_VMEM_BYTES),
        cost_estimate=pl.CostEstimate(
            flops=4 * count * v_own * inner * pixels,
            bytes_accessed=4 * inner * pixels + 12 * count * v_own * pixels,
            transcendentals=0,
        ),
        name="pixel_transform",
    )(*operands)


def signed_shift(freqs, length, step_size):
    centred = jnp.where(freqs >= length // 2, freqs - length, freqs)
    return jnp.floor_divide(centred, step_size)


def probe_windows(probe, shift_y, shift_x, lanes):
    grid_size = probe.shape[-1]
    stride = lanes // WIN
    count_x = shift_x.shape[0]
    n_rows = shift_y.shape[0] + WIN - stride
    rows = (shift_y[0] + jnp.arange(n_rows + stride - 1, dtype=jnp.int32)) % grid_size
    columns = (shift_x[:, None] + jnp.arange(WIN, dtype=jnp.int32)[None, :]) % grid_size
    picked = jnp.take(probe, rows, axis=1, mode="clip")
    chosen = (jnp.arange(grid_size, dtype=jnp.int32)[:, None] == columns.reshape(1, -1)).astype(jnp.float32)
    moved = jnp.einsum("prc,cm->prm", picked, chosen, precision=lax.Precision.HIGHEST)
    moved = moved.reshape(2, n_rows + stride - 1, count_x, WIN)
    return jnp.concatenate([moved[:, p : p + n_rows] for p in range(stride)], axis=-1)


def swap(array, partner, axis):
    size = lax.axis_size(axis)
    return lax.ppermute(array, axis, [(i, i ^ partner) for i in range(size)])


def gather_rows(block, axis):
    rank = lax.axis_index(axis)
    partner = 1
    while partner < lax.axis_size(axis):
        other = swap(block, partner, axis)
        ahead = (rank & partner) > 0
        block = jnp.concatenate(
            [jnp.where(ahead, other, block), jnp.where(ahead, block, other)], axis=1
        )
        partner *= 2
    return block


def shards(frames, probe_wave):
    n_grp, n_mem = lax.axis_size("grp"), lax.axis_size("mem")
    grp, mem = lax.axis_index("grp"), lax.axis_index("mem")
    n_y, n_x, pixels = frames.shape
    scan_y, scan_x = n_y * n_grp, n_x * n_mem
    u_own, v_own = scan_y // n_mem, scan_x // n_grp
    depth = min(LANES, pixels // n_grp)
    n_q = pixels // (n_grp * depth)
    partners = grp ^ jnp.arange(n_grp, dtype=jnp.int32)
    if n_x >= 32:
        opening = n_x // 4
        x_cuts = [(0, opening), (opening, n_x - opening)]
    else:
        x_cuts = [(0, n_x)]

    if u_own >= 8 * U_TILE:
        sizes = [u_own * 3 // 8, u_own // 4, u_own // 4, u_own // 8]
    else:
        sizes = [u_own // 2, u_own // 2]
    u_chunks = []
    for size in sizes:
        u_chunks.append((sum(c for _, c in u_chunks), size))

    def cut(q, first, count):
        made = []
        for j in range(n_grp - 1, -1, -1):
            at = (q * n_grp + (grp ^ j)) * depth
            piece = lax.dynamic_slice(frames, (0, first, at), (n_y, count, depth))
            made.append(piece.transpose(1, 0, 2))
        return made[::-1]

    def exchange(pieces):
        far = [swap(pieces[j], j, "grp") for j in range(n_grp - 1, 0, -1)]
        return [pieces[0]] + far[::-1]

    def to_owners(array):
        return lax.all_to_all(array, "mem", split_axis=0, concat_axis=0, tiled=True)

    def chosen(table, index, axis):
        return jnp.take(jnp.asarray(table), index, axis=axis, mode="clip")

    ty = chosen(y_table(scan_y).reshape(2 * scan_y, n_grp, n_y), partners, 1)
    ty = ty.reshape(2 * scan_y, scan_y)

    fronts = [(q, first, count) for q in range(n_q - 1) for first, count in x_cuts]
    fronts.append((n_q - 1, 0, n_x))
    halves = [u_chunks[0], (u_chunks[0][1], u_own - u_chunks[0][1])]
    pieces = cut(*fronts[0])
    pieces[n_grp // 2 :], probe_wave = lax.optimization_barrier((pieces[n_grp // 2 :], probe_wave))
    pieces = exchange(pieces)
    whole_probe = gather_rows(probe_wave, "mem")
    arrived = []
    for i in range(len(fronts) - 1):
        chunks = halves if i == len(fronts) - 2 else [(0, u_own)]
        ready = y_transform(ty, pieces, n_mem, chunks)
        following = cut(*fronts[i + 1])
        ready, following, whole_probe, arrived = lax.optimization_barrier(
            (ready, following, whole_probe, arrived)
        )
        arrived.append(to_owners(ready[0]))
        pieces = exchange(following)

    shift_y = signed_shift(
        mem * u_own + STRIDE_Y * jnp.arange(u_own // STRIDE_Y, dtype=jnp.int32), scan_y, STRIDE_Y
    )
    shift_x = signed_shift(grp * v_own + jnp.arange(v_own, dtype=jnp.int32), scan_x, STRIDE_X)
    base = whole_probe[:, :WIN, :WIN].reshape(2, WIN * WIN // LANES, LANES)
    windows = probe_windows(whole_probe, shift_y, shift_x, LANES)
    chi_table = jnp.asarray(pixel_table(WIN, LANES).reshape(2 * pixels, 2 * pixels))
    factors = chi_factors(windows, base, chi_table, u_own // STRIDE_Y)
    tx, tx_late = (
        chosen(x_table(scan_x, n_grp, n_mem, cuts), partners, 0).reshape(2 * scan_x, 2 * scan_x)
        for cuts in (x_cuts, [(0, n_x)])
    )
    blocks = (jnp.arange(n_q, dtype=jnp.int32)[:, None] * n_grp + partners[None, :]).reshape(-1)
    tk = chosen(pixel_table(WIN, depth), blocks, 0).reshape(2 * pixels, 2 * pixels)

    early = []
    late = []
    if fronts[:-1]:
        arrived, pending, factors, tx, pieces = lax.optimization_barrier((arrived, ready[1], factors, tx, pieces))
        last = to_owners(pending)
        late_ready = y_transform(ty, pieces, n_mem, u_chunks)
        sources = [(0, a) for a in arrived]
        early.append(exchange(x_transform(tx, sources, *halves[0], n_grp)))
        late_ready, last, tk, tx_late, early[0] = lax.optimization_barrier(
            (late_ready, last, tk, tx_late, early[0])
        )
        sources = sources[:-1] + [(halves[1][0], last)]
        last = to_owners(late_ready[0])
        early.append(exchange(x_transform(tx, sources, *halves[1], n_grp)))
    else:
        late_ready = y_transform(ty, pieces, n_mem, u_chunks)
        last = to_owners(late_ready[0])

    def early_of(first):
        return [(start, p) for (start, size), part in zip(halves, early) if start <= first < start + size for p in part]

    inner = 2 * pixels // n_q
    def finish(c, outs):
        first, count = u_chunks[c]
        own = [(first, p) for p in late[c]]
        if partials[c]:
            return pixel_transform(tk, inner, own, factors, partials[c], first, count, u_own, outs)
        return pixel_transform(tk, 0, early_of(first) + own, factors, [], first, count, u_own, outs)

    outs = []
    partials = [[] for _ in u_chunks]
    for c in range(1, len(u_chunks)):
        sending, last, early, late, partials, outs = lax.optimization_barrier(
            (late_ready[c], last, early, late, partials, outs)
        )
        following = to_owners(sending)
        first, count = u_chunks[c - 1]
        late.append(exchange(x_transform(tx_late, [(first, last)], first, count, n_grp)))
        last = following
        if c == 1 and early:
            for later in range(len(u_chunks) - 2, len(u_chunks)):
                first, count = u_chunks[later]
                partials[later] = pixel_transform(tk, 0, early_of(first), [], [], first, count, u_own, [])
        if c >= 2:
            outs = finish(c - 2, outs)
    last, partials, outs = lax.optimization_barrier((last, partials, outs))
    first, count = u_chunks[-1]
    late.append(exchange(x_transform(tx_late, [(first, last)], first, count, n_grp)))
    for c in range(max(0, len(u_chunks) - 2), len(u_chunks)):
        outs = finish(c, outs)
    return tuple(outs)


def solution(mesh):
    return jax.shard_map(
        shards,
        mesh=mesh,
        in_specs=(P("grp", "mem", None), P(None, "mem", None)),
        out_specs=(P("mem", "grp", None), P("mem", "grp", None)),
        check_vma=False,
    )
```
